32 devices in a mesh: dp: 8 (over z, y), tensor: 4 (over x, core).
Axes of the slice: x: 2, y: 2, z: 4, core: 2. Of those that a mesh axis runs over, the one named last changes fastest.
Arguments:
- queries: bfloat16 [4096, 4096], P('dp', 'tensor'), may hold values from -6 to 6
- passages: bfloat16 [2048, 4096], P('dp', 'tensor'), may hold values from -6 to 6
- neg_lists: int32 [64, 16], replicated, may hold values from -1 to 127, as said below
- positives: int32 [4096], P('dp'), may hold values from 0 to 2047, as said below
Outputs:
- query_grad: bfloat16 [4096, 4096], P('dp', 'tensor')
- passage_grad: bfloat16 [2048, 4096], P('dp', 'tensor')
- query_loss: float32 [4096], P('dp')
The draws below stay inside these ranges and needn't reach their ends.
Inputs may be any that keep to these rules, and one draw needn't show every extreme that they name: `neg_lists`: each row names distinct blocks, its live entries first and then -1, with 8 or more live. The rows of query blocks d * 8 to (d + 1) * 8 - 1 name at most 64 distinct blocks, and at most 8 distinct blocks of one owner, blocks d * 16 to (d + 1) * 16 - 1 belonging to index d of dp. `positives`: the positive of a query is a passage of a live block in its query block's row.
All inputs are finite; a program needn't handle non-finite values.
Results may differ from the reference program's by a relative error of at most 0.0051.
Values may be sent and summed in bfloat16 or wider, within the bound.
A program may use at most 128 MiB of HBM per device.

```python
import jax
import jax.numpy as jnp
from jax import lax

D = 4096
MINP = 64
NPRE = 7
QBLK = 64
NEG = 16
PBLK = 16
QBD = 8
PBD = 16
POOL = 64
CAP = 8
NQB = 64
NPB = 128
NQ = 4096
NP = 2048


def draw_structure(key):
    base_key = jax.random.fold_in(key, 17)
    owner_count = POOL // CAP

    def one_index(dp_index):
        index_key = jax.random.fold_in(base_key, dp_index)
        key_owner, key_start, key_first, key_second, key_counts, key_shuffle, key_pick, key_offset = jax.random.split(index_key, 8)
        owners = jax.random.permutation(key_owner, jnp.arange(POOL, dtype=jnp.int32) % owner_count)
        start = jax.random.randint(key_start, (owner_count,), 0, PBD, dtype=jnp.int32)
        pool_order = jnp.arange(POOL, dtype=jnp.int32)
        occurrence = jnp.sum(((owners[None, :] == owners[:, None]) & (pool_order[None, :] < pool_order[:, None])).astype(jnp.int32), axis=1)
        pool_ids = owners * PBD + (start[owners] + occurrence) % PBD
        first_half = pool_ids[jax.random.permutation(key_first, POOL)]
        second_half = pool_ids[jax.random.permutation(key_second, POOL)]
        list_rows = jnp.concatenate([first_half, second_half]).reshape(QBD, NEG)
        counts = jnp.concatenate([jax.random.randint(key_counts, (QBD // 2,), NEG // 2, NEG + 1, dtype=jnp.int32), jnp.full((QBD // 2,), NEG, jnp.int32)])
        keep_mask = jnp.arange(NEG, dtype=jnp.int32)[None, :] < counts[:, None]
        list_rows = jnp.where(keep_mask, list_rows, -1)
        shuffle = jax.random.permutation(key_shuffle, QBD)
        list_rows = list_rows[shuffle]
        counts = counts[shuffle]
        picked = jax.random.randint(key_pick, (QBD, QBLK), 0, counts[:, None], dtype=jnp.int32)
        offset = jax.random.randint(key_offset, (QBD, QBLK), 0, PBLK, dtype=jnp.int32)
        chosen = jnp.take_along_axis(list_rows, picked, axis=1)
        positive = chosen * PBLK + offset
        return (list_rows, positive.reshape(QBD * QBLK))
    list_rows, positive = jax.vmap(one_index)(jnp.arange(owner_count, dtype=jnp.int32))
    return (list_rows.reshape(NQB, NEG), positive.reshape(NQ))


def draw_neg_lists(key, part):
    return draw_structure(key)[0]


def draw_positives(key, part):
    return draw_structure(key)[1]


def block_scale(own_key, extent, cuts, smallest, high):
    level, own = 1.0, jax.random.fold_in(own_key, 6)
    for position, shards_of in cuts:
        steps = jnp.exp(jax.random.uniform(jax.random.fold_in(own, position), (shards_of,), jnp.float32, smallest / len(cuts), high / len(cuts)))
        level = level * jnp.repeat(steps, extent[position] // shards_of).reshape([-1 if axis == position else 1 for axis in range(len(extent))])
    return level


def scatter_about(rng, dims, width, bound, pieces=(), kind=jnp.bfloat16):
    gain = block_scale(rng, dims, pieces, -0.22, 0.18) if pieces else 1.0
    array = jax.random.normal(rng, dims, jnp.float32) * width * gain
    return jnp.minimum(jnp.maximum(array, -bound), bound).astype(kind)


def setup_inputs(seed: int = 0) -> dict:
    seeds = jax.random.split(jax.random.key(seed), 5)
    queries = scatter_about(seeds[0], (NQ, D), 1.0, 6.0, ((0, 8), (1, 4)))
    passages = scatter_about(seeds[1], (NP, D), 1.0, 6.0, ((0, 8), (1, 4)))
    neg_lists = draw_neg_lists(jax.random.fold_in(seeds[4], 71), 0)
    positives = draw_positives(jax.random.fold_in(seeds[4], 71), 0)
    return {"queries": queries, "passages": passages, "neg_lists": neg_lists, "positives": positives}


EPS = 1e-06
INV_TEMP = 20.0

def prefix_terms(dot_sums, query_sq, passage_sq, cand_mask, labels, weight):
    query_scale = lax.rsqrt(query_sq + EPS)
    passage_scale = jnp.where(cand_mask, lax.rsqrt(passage_sq + EPS), 0.0)
    logits = dot_sums * query_scale[..., :, None] * passage_scale[..., None, :] * INV_TEMP
    exponent = jnp.where(cand_mask[..., None, :], jnp.exp(logits), 0.0)
    exp_total = lax.optimization_barrier(jnp.sum(exponent, axis=-1))
    probability = exponent / exp_total[..., None]
    cross_entropy = jnp.log(exp_total) - lax.optimization_barrier(jnp.sum(labels * logits, axis=-1))
    gradient = weight * (probability - labels)
    coefficient = gradient * query_scale[..., :, None] * passage_scale[..., None, :] * INV_TEMP
    inner_term = gradient * logits
    row_term = jnp.square(query_scale) * lax.optimization_barrier(jnp.sum(inner_term, axis=-1))
    col_term = jnp.square(passage_scale) * lax.optimization_barrier(jnp.sum(inner_term, axis=-2))
    return (coefficient, row_term, col_term, weight * cross_entropy)

def reference(queries, passages, neg_lists, positives):
    prefix_sizes = [MINP * 2 ** level_index for level_index in range(NPRE)]
    bounds = [0] + prefix_sizes
    weight_total = sum((prefix_size / MINP for prefix_size in prefix_sizes))
    query_blocks = queries.reshape(NQB, QBLK, D)
    passage_blocks = passages.reshape(NPB, PBLK, D)
    positive_rows = positives.reshape(NQB, QBLK)
    within_block = jnp.arange(PBLK, dtype=jnp.int32)
    cand_count = NEG * PBLK

    def one_block(accumulated, item_data):
        query_block, block_row, positive_row = item_data
        is_valid = block_row >= 0
        safe_row = jnp.where(is_valid, block_row, 0).astype(jnp.int32)
        candidates = jnp.where(is_valid[:, None, None], passage_blocks[safe_row], jnp.zeros((), jnp.bfloat16))
        candidates = candidates.reshape(cand_count, D)
        cand_mask = jnp.repeat(is_valid, PBLK)
        cand_ids = (safe_row[:, None] * PBLK + within_block[None, :]).reshape(cand_count)
        labels = ((cand_ids[None, :] == positive_row[:, None]) & cand_mask[None, :]).astype(jnp.float32)
        dot_sums = jnp.zeros((QBLK, cand_count), jnp.float32)
        query_sq = jnp.zeros((QBLK,), jnp.float32)
        passage_sq = jnp.zeros((cand_count,), jnp.float32)
        coef_list, row_list, col_list = ([], [], [])
        loss_sum = jnp.zeros((QBLK,), jnp.float32)
        for level_index in range(NPRE):
            low_col, high_col = (bounds[level_index], bounds[level_index + 1])
            query_seg = query_block[:, low_col:high_col]
            passage_seg = candidates[:, low_col:high_col]
            dot_sums = dot_sums + jnp.dot(query_seg, passage_seg.T, preferred_element_type=jnp.float32)
            query_sq = query_sq + lax.optimization_barrier(jnp.sum(jnp.square(query_seg.astype(jnp.float32)), axis=1))
            passage_sq = passage_sq + lax.optimization_barrier(jnp.sum(jnp.square(passage_seg.astype(jnp.float32)), axis=1))
            coefficient, row_term, col_term, weighted = prefix_terms(dot_sums, query_sq, passage_sq, cand_mask, labels, prefix_sizes[level_index] / MINP)
            coef_list.append(coefficient)
            row_list.append(row_term)
            col_list.append(col_term)
            loss_sum = loss_sum + weighted
        sum_coef = jnp.zeros((QBLK, cand_count), jnp.float32)
        sum_row = jnp.zeros((QBLK,), jnp.float32)
        sum_col = jnp.zeros((cand_count,), jnp.float32)
        query_parts, passage_parts = ([], [])
        for level_index in reversed(range(NPRE)):
            sum_coef = sum_coef + coef_list[level_index]
            sum_row = sum_row + row_list[level_index]
            sum_col = sum_col + col_list[level_index]
            low_col, high_col = (bounds[level_index], bounds[level_index + 1])
            query_seg = query_block[:, low_col:high_col]
            passage_seg = candidates[:, low_col:high_col]
            coef_half = sum_coef.astype(jnp.bfloat16)
            query_parts.append(jnp.dot(coef_half, passage_seg, preferred_element_type=jnp.float32) - sum_row[:, None] * query_seg.astype(jnp.float32))
            passage_parts.append(jnp.dot(coef_half.T, query_seg, preferred_element_type=jnp.float32) - sum_col[:, None] * passage_seg.astype(jnp.float32))
        query_grad = jnp.concatenate(query_parts[::-1], axis=1).astype(jnp.bfloat16)
        cand_grad = jnp.concatenate(passage_parts[::-1], axis=1).reshape(NEG, PBLK, D)
        cand_grad = jnp.where(is_valid[:, None, None], cand_grad, 0.0)
        accumulated = accumulated.at[safe_row].add(cand_grad)
        return (accumulated, (query_grad, loss_sum / weight_total))
    start_grad = jnp.zeros((NPB, PBLK, D), jnp.float32)
    passage_total, outputs = lax.scan(one_block, start_grad, (query_blocks, neg_lists, positive_rows))
    query_grad, query_loss = outputs
    return (query_grad.reshape(NQ, D), passage_total.reshape(NP, D).astype(jnp.bfloat16), query_loss.reshape(NQ))
```

```python
from functools import partial

import jax
import jax.numpy as jnp
from jax import lax
from jax.experimental import pallas as pl
from jax.experimental.pallas import tpu as pltpu
from jax.sharding import PartitionSpec as P

MINP = 64
NPRE = 7
PBLK = 16
QBLK = 64
LANES = 128
OWN = 5

EPS = 1e-06
INV_TEMP = 20.0
MESH = pl.DeviceIdType.MESH
F32 = jnp.float32
BF16 = jnp.bfloat16


def request_plan(flat_ids, capacity, per_owner):
    entry_count = flat_ids.shape[0]
    is_valid = flat_ids >= 0
    entry_order = jnp.arange(entry_count, dtype=jnp.int32)
    earlier = entry_order[None, :] < entry_order[:, None]
    same_block = (flat_ids[:, None] == flat_ids[None, :]) & is_valid[None, :]
    is_first = is_valid & jnp.logical_not(jnp.any(same_block & earlier, axis=1))
    owner_index = jnp.where(is_valid, flat_ids // per_owner, 0)
    local_block = jnp.where(is_valid, flat_ids % per_owner, 0)
    owner_rank = jnp.sum(
        ((owner_index[:, None] == owner_index[None, :]) & earlier & is_first[None, :]).astype(
            jnp.int32
        ),
        axis=1,
    )
    home_slot = jnp.where(is_first, owner_index * capacity + owner_rank, 0)
    entry_slot = jnp.sum(jnp.where(same_block & is_first[None, :], home_slot[None, :], 0), axis=1)
    return (is_first, home_slot, entry_slot, local_block)


def dot_nt(left, right):
    return lax.dot_general(left, right, (((1,), (1,)), ((), ())), preferred_element_type=F32)


def dot_tn(left, right):
    return lax.dot_general(left, right, (((0,), (0,)), ((), ())), preferred_element_type=F32)


def to_row(column):
    return column.T[0:1, :]


def to_column(row):
    return jnp.broadcast_to(row, (LANES, LANES)).T


def kernel(
    peers, cap, blocks, neg, local_blocks,
    tab, pos_ref, q_ref, p_ref, dq_ref, dp_ref, loss_ref,
    panels, sendbuf, gradbuf, returned, dots, psq, cid, gathered, got, coef, terms, half,
    grid, cols, qsq, rows, small, got_small, back, got_back,
    send1, recv1, send2, recv2, dg_send, dg_recv, sm_send, sm_recv, cf_send, cf_recv,
    sb_send, sb_recv,
):
    me, shard = lax.axis_index("dp"), lax.axis_index("tensor")
    width = q_ref.shape[1]
    chunk = cap * PBLK
    slots = peers * cap
    pairs = blocks // 2
    cand = neg * PBLK
    tiles = slots * PBLK // LANES
    want_at = 0
    slot_at = want_at + slots
    id_at = slot_at + blocks * neg
    ent_at = id_at + blocks * neg
    inv_at = ent_at + blocks * slots
    last = OWN - 1

    barrier = pltpu.get_barrier_semaphore()

    def greet(step, carry):
        pl.semaphore_signal(
            barrier, inc=1, device_id={"dp": lax.rem(me + step, peers)}, device_id_type=MESH
        )
        return carry

    lax.fori_loop(1, peers, greet, 0)
    for step in range(1, 4):
        pl.semaphore_signal(
            barrier, inc=1, device_id={"tensor": lax.rem(shard + step, 4)}, device_id_type=MESH
        )

    def pack(peer, target, offset):
        for k in range(cap):
            block = tab[want_at + peer * cap + k]
            target[pl.ds(offset + k * PBLK, PBLK), :] = p_ref[pl.ds(block * PBLK, PBLK), :]

    def chunk_rows(peer):
        return pl.ds(pl.multiple_of(peer * chunk, PBLK), chunk)

    def fetch(peer):
        return pltpu.make_async_remote_copy(
            src_ref=sendbuf.at[chunk_rows(peer)],
            dst_ref=panels.at[chunk_rows(me)],
            send_sem=send1.at[peer],
            recv_sem=recv1.at[me],
            device_id={"dp": peer},
            device_id_type=MESH,
        )

    def fetched(peer):
        return pltpu.make_async_remote_copy(
            src_ref=sendbuf.at[chunk_rows(me)],
            dst_ref=panels.at[chunk_rows(peer)],
            send_sem=send1.at[me],
            recv_sem=recv1.at[peer],
            device_id={"dp": peer},
            device_id_type=MESH,
        )

    pl.semaphore_wait(barrier, peers - 1 + 3)

    def start_fetch(step, carry):
        peer = lax.rem(me + step, peers)
        pack(peer, sendbuf, pl.multiple_of(peer * chunk, PBLK))
        fetch(peer).start()
        return carry

    lax.fori_loop(1, peers, start_fetch, 0)
    pack(me, panels, pl.multiple_of(me * chunk, PBLK))

    low_half = lax.broadcasted_iota(jnp.int32, (PBLK, LANES), 1) < QBLK
    low_row = lax.broadcasted_iota(jnp.int32, (1, LANES), 1) < QBLK

    def query_terms(j, carry):
        block = q_ref[pl.ds(pl.multiple_of(j * LANES, LANES), LANES), :].astype(F32)
        square = block * block

        def put(k, value):
            qsq[k, pl.ds(j, 1), :] = to_row(jnp.broadcast_to(value, (LANES, LANES)))

        prefix_squares(square, put)
        for e in range(neg):
            low = tab[id_at + (2 * j) * neg + e]
            high = tab[id_at + (2 * j + 1) * neg + e]
            cid[j, e * PBLK : (e + 1) * PBLK, :] = jnp.where(
                low_half, low, high
            ) * PBLK + lax.broadcasted_iota(jnp.int32, (PBLK, LANES), 0)
        return carry

    def prefix_squares(square, put):
        @pl.when(shard == 0)
        def _():
            first = square[:, :LANES]
            total = jnp.sum(jnp.where(low_row, first, 0.0), axis=1, keepdims=True)
            put(0, total)
            total = jnp.sum(first, axis=1, keepdims=True)
            put(1, total)
            for k in range(2, OWN):
                total = total + jnp.sum(
                    square[:, MINP * 2 ** (k - 1) : MINP * 2**k], axis=1, keepdims=True
                )
                put(k, total)

        @pl.when(shard != 0)
        def _():
            put(last, jnp.sum(square, axis=1, keepdims=True))

    lax.fori_loop(0, pairs, query_terms, 0)

    for k in range(OWN):
        half[k, :, cand : cand + PBLK, :] = jnp.zeros((pairs, PBLK, LANES), BF16)
        terms[k, :, cand : cand + PBLK, :] = jnp.zeros((pairs, PBLK, LANES), F32)
    back[...] = jnp.zeros_like(back)
    small[...] = jnp.zeros_like(small)

    def forward(step, carry):
        peer = lax.rem(me + step, peers)

        @pl.when(step > 0)
        def _():
            fetched(peer).wait_recv()

        here = chunk_rows(peer)
        square = panels[here, :].astype(F32)
        square = square * square

        def put(k, value):
            psq[k, here, :] = jnp.broadcast_to(value, (chunk, LANES))

        prefix_squares(square, put)

        def keep(k, value):
            for j in range(pairs):
                dots[k, j, here, :] = value[:, j * LANES : (j + 1) * LANES]

        @pl.when(shard == 0)
        def _():
            first, query = panels[here, :LANES], q_ref[:, :LANES]
            keep(0, dot_nt(jnp.where(low_row, first, jnp.zeros((), BF16)), query))
            total = dot_nt(first, query)
            keep(1, total)
            for k in range(2, OWN):
                span = slice(MINP * 2 ** (k - 1), MINP * 2**k)
                total = total + dot_nt(panels[here, span], q_ref[:, span])
                keep(k, total)

        @pl.when(shard != 0)
        def _():
            keep(last, dot_nt(panels[here, :], q_ref[...]))

        return carry

    lax.fori_loop(0, peers, forward, 0)

    def pick(ref, k, j, lead):
        parts = []
        for e in range(neg):
            low = tab[slot_at + (2 * j) * neg + e] * PBLK
            high = tab[slot_at + (2 * j + 1) * neg + e] * PBLK
            low = ref[lead(k, j) + (pl.ds(low, PBLK),)]
            high = ref[lead(k, j) + (pl.ds(high, PBLK),)]
            parts.append(jnp.where(low_half, low, high))
        return jnp.concatenate(parts, axis=0)

    def pick_dots(k, j):
        return pick(dots, k, j, lambda k, j: (k, j))

    def pick_squares(k, j):
        return pick(psq, k, j, lambda k, j: (k,))

    def small_copy(target, slot):
        return pltpu.make_async_remote_copy(
            src_ref=small, dst_ref=got_small.at[slot], send_sem=sm_send.at[0],
            recv_sem=sm_recv.at[slot], device_id={"tensor": target}, device_id_type=MESH,
        )

    def dots_copy(target, slot, j):
        return pltpu.make_async_remote_copy(
            src_ref=gathered.at[j], dst_ref=got.at[slot, j], send_sem=dg_send.at[j],
            recv_sem=dg_recv.at[slot, j], device_id={"tensor": target}, device_id_type=MESH,
        )

    def later_copy(j):
        return pltpu.make_async_remote_copy(
            src_ref=coef.at[last, j], dst_ref=got.at[0, j], send_sem=cf_send.at[0, j],
            recv_sem=dg_recv.at[0, j], device_id={"tensor": 0}, device_id_type=MESH,
        )

    def half_copy(target, j):
        return pltpu.make_async_remote_copy(
            src_ref=half.at[last, j, pl.ds(0, cand)], dst_ref=half.at[last, j, pl.ds(0, cand)],
            send_sem=cf_send.at[target - 1, j], recv_sem=cf_recv.at[j],
            device_id={"tensor": target}, device_id_type=MESH,
        )

    for t in range(tiles):
        small[t : t + 1, :] = to_row(psq[last, t * LANES : (t + 1) * LANES, :])
    small[tiles : tiles + pairs, :] = qsq[last, 0:pairs, :]

    def widen():
        for t in range(tiles):
            psq[last, t * LANES : (t + 1) * LANES, :] = to_column(small[t : t + 1, :])
        qsq[last, 0:pairs, :] = small[tiles : tiles + pairs, :]

    def each_pair(body):
        def step(j, carry):
            body(j)
            return carry

        lax.fori_loop(0, pairs, step, 0)

    def prefix_terms(products, squares, k, j, weight):
        number = cid[j]
        live = number >= 0
        query_scale = lax.rsqrt(qsq[k, pl.ds(j, 1), :] + EPS)
        passage_scale = jnp.where(live, lax.rsqrt(squares + EPS), 0.0)
        scale = query_scale * passage_scale * INV_TEMP
        logits = products * scale
        exponent = jnp.where(live, jnp.exp(logits), 0.0)
        total = jnp.sum(exponent, axis=0, keepdims=True)
        hit = number == pos_ref[pl.ds(j, 1), :]
        loss = jnp.log(total) - jnp.sum(jnp.where(hit, logits, 0.0), axis=0, keepdims=True)
        gradient = weight * (exponent * (1.0 / total) - jnp.where(hit, 1.0, 0.0))
        inner = gradient * logits
        row = query_scale * query_scale * jnp.sum(inner, axis=0, keepdims=True)
        return gradient * scale, row, passage_scale * passage_scale * inner, weight * loss

    def one_prefix(products, j, weight):
        value, row, column, loss = prefix_terms(
            products, pick_squares(last, j), last, j, weight
        )
        coef[last, j] = value
        terms[last, j, 0:cand, :] = column
        rows[last, pl.ds(j, 1), :] = row
        back[pl.ds(tiles + pairs + j, 1), :] = loss

    def pick_half(ref, k, j, slot):
        low = tab[ent_at + (2 * j) * slots + slot] * PBLK
        high = tab[ent_at + (2 * j + 1) * slots + slot] * PBLK
        return jnp.where(
            low_half,
            ref[k, j, pl.ds(low, PBLK), :],
            ref[k, j, pl.ds(high, PBLK), :],
        )

    def column_sums(count):
        def step(slot, carry):
            for k in range(OWN - count, OWN):
                total = pick_half(terms, k, 0, slot)
                for j in range(1, pairs):
                    total = total + pick_half(terms, k, j, slot)
                cols[k, pl.ds(pl.multiple_of(slot * PBLK, PBLK), PBLK), :] = jnp.broadcast_to(
                    jnp.sum(total, axis=1, keepdims=True), (PBLK, LANES)
                )
            return carry

        lax.fori_loop(0, slots, step, 0)
        for t in range(tiles):
            back[t : t + 1, :] = to_row(cols[last, t * LANES : (t + 1) * LANES, :])
        back[tiles : tiles + pairs, :] = rows[last, 0:pairs, :]

    def back_copy(step, slot):
        return pltpu.make_async_remote_copy(
            src_ref=back, dst_ref=got_back.at[slot], send_sem=sb_send.at[step],
            recv_sem=sb_recv.at[slot], device_id={"tensor": lax.rem(shard + step, 4)},
            device_id_type=MESH,
        )

    def send_back():
        for step in range(1, 4):
            back_copy(step, shard).start()

    @pl.when(shard == 0)
    def _():
        small_copy(1, 0).start()

        def hand_on(j):
            gathered[j] = pick_dots(last, j)
            dots_copy(1, 0, j).start()

        each_pair(hand_on)

        def own(j):
            value = row = column = loss = None
            for k in reversed(range(OWN)):
                products = gathered[j] if k == last else pick_dots(k, j)
                part = prefix_terms(products, pick_squares(k, j), k, j, float(2**k))
                if k == last:
                    value, row, column, loss = part
                else:
                    value, row, column, loss = (
                        value + part[0], row + part[1], column + part[2], loss + part[3]
                    )
                coef[k, j] = value
                rows[k, pl.ds(j, 1), :] = row
                terms[k, j, 0:cand, :] = column
            back[pl.ds(tiles + pairs + j, 1), :] = loss

        each_pair(own)
        column_sums(OWN)
        send_back()

        def finish(j):
            later_copy(j).wait_recv()
            for k in range(OWN):
                half[k, j, 0:cand, :] = (coef[k, j] + got[0, j]).astype(BF16)

        each_pair(finish)
        small_copy(1, 0).wait_send()
        each_pair(lambda j: dots_copy(1, 0, j).wait_send())

    @pl.when(shard == 1)
    def _():
        small_copy(3, 0).wait_recv()
        small[...] = small[...] + got_small[0]
        small_copy(3, 0).start()

        def hand_on(j):
            dots_copy(3, 0, j).wait_recv()
            gathered[j] = pick_dots(last, j) + got[0, j]
            dots_copy(3, 0, j).start()

        each_pair(hand_on)
        widen()
        each_pair(lambda j: one_prefix(gathered[j], j, 32.0))
        column_sums(1)
        send_back()

        def finish(j):
            half_copy(1, j).wait_recv()
            total = coef[last, j] + half[last, j, 0:cand, :].astype(F32)
            coef[last, j] = total
            later_copy(j).start()
            half[last, j, 0:cand, :] = total.astype(BF16)

        each_pair(finish)
        small_copy(3, 0).wait_send()
        each_pair(lambda j: dots_copy(3, 0, j).wait_send())
        each_pair(lambda j: later_copy(j).wait_send())

    @pl.when(shard == 2)
    def _():
        small_copy(3, 1).start()

        def hand_on(j):
            gathered[j] = pick_dots(last, j)
            dots_copy(3, 1, j).start()

        each_pair(hand_on)
        cols[last] = jnp.zeros_like(cols[last])
        rows[last] = jnp.zeros_like(rows[last])
        send_back()
        each_pair(lambda j: half_copy(2, j).wait_recv())
        small_copy(3, 1).wait_send()
        each_pair(lambda j: dots_copy(3, 1, j).wait_send())

    @pl.when(shard == 3)
    def _():
        small_copy(2, 0).wait_recv()
        small_copy(2, 1).wait_recv()
        small[...] = small[...] + got_small[0] + got_small[1]
        widen()

        def answer(j):
            mine = pick_dots(last, j)
            dots_copy(2, 1, j).wait_recv()
            dots_copy(2, 0, j).wait_recv()
            one_prefix(mine + got[0, j] + got[1, j], j, 64.0)
            half[last, j, 0:cand, :] = coef[last, j].astype(BF16)
            half_copy(1, j).start()
            half_copy(2, j).start()

        each_pair(answer)
        column_sums(1)
        send_back()
        each_pair(lambda j: half_copy(1, j).wait_send())
        each_pair(lambda j: half_copy(2, j).wait_send())

    later = jnp.zeros(back.shape, F32)
    loss = back[tiles + pairs : tiles + 2 * pairs, :]
    for step in range(1, 4):
        other = lax.rem(shard + step, 4)
        back_copy(step, other).wait_recv()
        part = got_back[other]
        later = later + jnp.where(other > shard, 1.0, 0.0) * part
        loss = loss + part[tiles + pairs : tiles + 2 * pairs, :]
    weight_total = sum(2.0**k for k in range(NPRE))
    loss_ref[...] = loss / weight_total

    def add_later(count):
        for t in range(tiles):
            extra = to_column(later[t : t + 1, :])
            for k in range(OWN - count, OWN):
                cols[k, t * LANES : (t + 1) * LANES, :] += extra
        for k in range(OWN - count, OWN):
            rows[k, 0:pairs, :] += later[tiles : tiles + pairs, :]

    @pl.when(shard == 0)
    def _():
        add_later(OWN)

    @pl.when(shard != 0)
    def _():
        add_later(1)

    spans = [(k, slice(MINP * 2 ** (k - 1), MINP * 2**k)) for k in range(2, OWN)]

    def build(k, peer):
        def step(i, carry):
            slot = peer * cap + i
            for j in range(pairs):
                grid[
                    k, pl.ds(pl.multiple_of(slot * PBLK, PBLK), PBLK), j * LANES : (j + 1) * LANES
                ] = pick_half(half, k, j, slot)
            return carry

        lax.fori_loop(0, cap, step, 0)

    def send_grad(peer):
        return pltpu.make_async_remote_copy(
            src_ref=gradbuf.at[chunk_rows(peer)], dst_ref=returned.at[me, pl.ds(0, chunk)],
            send_sem=send2.at[peer], recv_sem=recv2.at[me],
            device_id={"dp": peer}, device_id_type=MESH,
        )

    def came_back(peer):
        return pltpu.make_async_remote_copy(
            src_ref=gradbuf.at[chunk_rows(me)], dst_ref=returned.at[peer, pl.ds(0, chunk)],
            send_sem=send2.at[me], recv_sem=recv2.at[peer],
            device_id={"dp": peer}, device_id_type=MESH,
        )

    def passage_part(step, carry):
        peer = lax.rem(me + step, peers)
        here = chunk_rows(peer)

        def put(span, k, product):
            piece = product - cols[k, here, 0:1] * panels[here, span].astype(F32)
            gradbuf[here, span] = piece.astype(BF16)

        @pl.when(shard == 0)
        def _():
            for k in range(OWN):
                build(k, peer)
            query = q_ref[:, :LANES]
            first = panels[here, :LANES].astype(F32)
            low = jnp.dot(grid[0, here, :], query, preferred_element_type=F32)
            low = low - cols[0, here, :] * first
            high = jnp.dot(grid[1, here, :], query, preferred_element_type=F32)
            high = high - cols[1, here, :] * first
            gradbuf[here, :LANES] = jnp.where(low_row, low, high).astype(BF16)
            for k, span in spans:
                put(span, k, jnp.dot(grid[k, here, :], q_ref[:, span], preferred_element_type=F32))

        @pl.when(shard != 0)
        def _():
            build(last, peer)
            put(
                slice(0, width), last,
                jnp.dot(grid[last, here, :], q_ref[...], preferred_element_type=F32),
            )

        @pl.when(step < peers)
        def _():
            send_grad(peer).start()

        @pl.when(step == peers)
        def _():
            returned[me, 0:chunk, :] = gradbuf[here, :]

        return carry

    lax.fori_loop(1, peers + 1, passage_part, 0)

    def query_part(j, carry):
        here = pl.ds(pl.multiple_of(j * LANES, LANES), LANES)

        def column(k):
            return to_column(rows[k, pl.ds(j, 1), :])

        def product(k, span):
            return dot_tn(grid[k, :, here], panels[:, span])

        @pl.when(shard == 0)
        def _():
            query = q_ref[here, :LANES].astype(F32)
            first = slice(0, LANES)
            low = product(0, first) - column(0) * query
            high = product(1, first) - column(1) * query
            dq_ref[here, :LANES] = jnp.where(low_row, low, high).astype(BF16)
            for k, span in spans:
                piece = product(k, span) - column(k)[:, 0:1] * q_ref[here, span].astype(F32)
                dq_ref[here, span] = piece.astype(BF16)

        @pl.when(shard != 0)
        def _():
            piece = product(last, slice(0, width)) - column(last)[:, 0:1] * q_ref[here, :].astype(F32)
            dq_ref[here, :] = piece.astype(BF16)

        return carry

    lax.fori_loop(0, pairs, query_part, 0)

    returned[:, chunk : chunk + PBLK, :] = jnp.zeros((peers, PBLK, width), BF16)

    def drain(step, carry):
        peer = lax.rem(me + step, peers)
        came_back(peer).wait_recv()
        return carry

    lax.fori_loop(1, peers, drain, 0)

    def total_block(block, carry):
        def add(peer, total):
            row = tab[inv_at + peer * local_blocks + block] * PBLK
            return total + returned[peer, pl.ds(row, PBLK), :].astype(F32)

        total = lax.fori_loop(0, peers, add, jnp.zeros((PBLK, width), F32))
        dp_ref[pl.ds(pl.multiple_of(block * PBLK, PBLK), PBLK), :] = total.astype(BF16)
        return carry

    lax.fori_loop(0, local_blocks, total_block, 0)

    def sent(step, carry):
        peer = lax.rem(me + step, peers)
        fetch(peer).wait_send()
        send_grad(peer).wait_send()
        return carry

    lax.fori_loop(1, peers, sent, 0)
    for step in range(1, 4):
        back_copy(step, shard).wait_send()


def per_device(queries, passages, neg_lists, positives):
    peer_count = lax.axis_size("dp")
    width = queries.shape[1]
    blocks_here = neg_lists.shape[0] // peer_count
    neg_count = neg_lists.shape[1]
    local_blocks = passages.shape[0] // PBLK
    capacity = blocks_here * neg_count // 2 // peer_count
    slot_count = peer_count * capacity
    cand = neg_count * PBLK
    pairs = blocks_here // 2
    my_index = lax.axis_index("dp")
    flat_all = neg_lists.reshape(peer_count, blocks_here * neg_count)
    is_first, home_slot, entry_slot, local_block = jax.vmap(
        partial(request_plan, capacity=capacity, per_owner=local_blocks)
    )(flat_all)
    targets = my_index * capacity + jnp.arange(capacity, dtype=jnp.int32)
    target_hit = is_first[:, :, None] & (home_slot[:, :, None] == targets[None, None, :])
    wanted = jnp.sum(jnp.where(target_hit, local_block[:, :, None] + 1, 0), axis=1) - 1
    own_ids = lax.dynamic_index_in_dim(flat_all, my_index, 0, keepdims=False)
    own_slot = lax.dynamic_index_in_dim(entry_slot, my_index, 0, keepdims=False)
    own_live = own_ids >= 0
    entries = jnp.arange(neg_count, dtype=jnp.int32)[None, :, None]
    at_slot = (
        own_slot.reshape(blocks_here, neg_count, 1) == jnp.arange(slot_count, dtype=jnp.int32)
    ) & own_live.reshape(blocks_here, neg_count, 1)
    entry_of = neg_count + jnp.sum(jnp.where(at_slot, entries - neg_count, 0), axis=1)
    named = wanted[:, :, None] == jnp.arange(local_blocks, dtype=jnp.int32)
    ranks = jnp.arange(capacity, dtype=jnp.int32)[None, :, None]
    rank_of = capacity + jnp.sum(jnp.where(named, ranks - capacity, 0), axis=1)
    table = jnp.concatenate([
        jnp.maximum(wanted, 0).reshape(-1),
        jnp.where(own_live, own_slot, 0),
        jnp.where(own_live, own_ids, -1),
        entry_of.reshape(-1),
        rank_of.reshape(-1),
    ]).astype(jnp.int32)

    slot_rows = slot_count * PBLK
    query_count = queries.shape[0]
    smalls = slot_rows // LANES + 2 * pairs
    vmem, dma = pltpu.VMEM, pltpu.SemaphoreType.DMA
    whole = pl.BlockSpec(memory_space=pltpu.VMEM)
    query_grad, passage_grad, loss = pl.pallas_call(
        partial(kernel, peer_count, capacity, blocks_here, neg_count, local_blocks),
        out_shape=(
            jax.ShapeDtypeStruct(queries.shape, BF16),
            jax.ShapeDtypeStruct(passages.shape, BF16),
            jax.ShapeDtypeStruct((pairs, LANES), F32),
        ),
        in_specs=[pl.BlockSpec(memory_space=pltpu.SMEM), whole, whole, whole],
        out_specs=(whole, whole, whole),
        scratch_shapes=[
            vmem((slot_rows, width), BF16),
            vmem((slot_rows, width), BF16),
            vmem((slot_rows, width), BF16),
            vmem((peer_count, (capacity + 1) * PBLK, width), BF16),
            vmem((OWN, pairs, slot_rows, LANES), F32),
            vmem((OWN, slot_rows, LANES), F32),
            vmem((pairs, cand, LANES), jnp.int32),
            vmem((pairs, cand, LANES), F32),
            vmem((2, pairs, cand, LANES), F32),
            vmem((OWN, pairs, cand, LANES), F32),
            vmem((OWN, pairs, cand + PBLK, LANES), F32),
            vmem((OWN, pairs, cand + PBLK, LANES), BF16),
            vmem((OWN, slot_rows, query_count), BF16),
            vmem((OWN, slot_rows, LANES), F32),
            vmem((OWN, 8, LANES), F32),
            vmem((OWN, 8, LANES), F32),
            vmem((smalls, LANES), F32),
            vmem((2, smalls, LANES), F32),
            vmem((smalls, LANES), F32),
            vmem((4, smalls, LANES), F32),
            dma((peer_count,)), dma((peer_count,)), dma((peer_count,)), dma((peer_count,)),
            dma((pairs,)), dma((2, pairs)), dma((1,)), dma((2,)),
            dma((2, pairs)), dma((pairs,)), dma((4,)), dma((4,)),
        ],
        compiler_params=pltpu.CompilerParams(
            collective_id=0, has_side_effects=True, vmem_limit_bytes=56 * 2**20
        ),
        name="matryoshka",
    )(table, positives.reshape(pairs, LANES), queries, passages)
    return query_grad, passage_grad, loss.reshape(query_count)


def solution(mesh):
    return jax.shard_map(
        per_device,
        mesh=mesh,
        in_specs=(P("dp", "tensor"), P("dp", "tensor"), P(), P("dp")),
        out_specs=(P("dp", "tensor"), P("dp", "tensor"), P("dp")),
        check_vma=False,
    )
```

```python
from functools import partial

import jax
import jax.numpy as jnp
from jax import lax
from jax.experimental import pallas as pl
from jax.experimental.pallas import tpu as pltpu
from jax.sharding import PartitionSpec as P

MINP = 64
NPRE = 7
PBLK = 16
QBLK = 64
LANES = 128
OWN = 5

EPS = 1e-06
INV_TEMP = 20.0
MESH = pl.DeviceIdType.MESH
F32 = jnp.float32
BF16 = jnp.bfloat16


def request_plan(flat_ids, capacity, per_owner):
    entry_count = flat_ids.shape[0]
    is_valid = flat_ids >= 0
    entry_order = jnp.arange(entry_count, dtype=jnp.int32)
    earlier = entry_order[None, :] < entry_order[:, None]
    same_block = (flat_ids[:, None] == flat_ids[None, :]) & is_valid[None, :]
    is_first = is_valid & jnp.logical_not(jnp.any(same_block & earlier, axis=1))
    owner_index = jnp.where(is_valid, flat_ids // per_owner, 0)
    local_block = jnp.where(is_valid, flat_ids % per_owner, 0)
    owner_rank = jnp.sum(
        ((owner_index[:, None] == owner_index[None, :]) & earlier & is_first[None, :]).astype(
            jnp.int32
        ),
        axis=1,
    )
    home_slot = jnp.where(is_first, owner_index * capacity + owner_rank, 0)
    entry_slot = jnp.sum(jnp.where(same_block & is_first[None, :], home_slot[None, :], 0), axis=1)
    return (is_first, home_slot, entry_slot, local_block)


def dot_nt(left, right):
    return lax.dot_general(left, right, (((1,), (1,)), ((), ())), preferred_element_type=F32)


def dot_tn(left, right):
    return lax.dot_general(left, right, (((0,), (0,)), ((), ())), preferred_element_type=F32)


def partner(me, step, peers):
    other, digit = 0, 1
    while digit < peers:
        other = other + lax.rem(lax.div(me, digit) + lax.div(step, digit), 2) * digit
        digit *= 2
    return other


def to_row(column):
    return column.T[0:1, :]


def to_column(row):
    return jnp.broadcast_to(row, (LANES, LANES)).T


def kernel(
    peers, cap, blocks, neg, local_blocks,
    tab, pos_ref, q_ref, p_ref, dq_ref, dp_ref, loss_ref,
    panels, sendbuf, gradbuf, returned, dots, psq, cid, gathered, got, coef, terms, half,
    grid, cols, qsq, rows, small, got_small, back, got_back,
    send1, recv1, send2, recv2, dg_send, dg_recv, sm_send, sm_recv, cf_send, cf_recv,
    sb_send, sb_recv,
):
    me, shard = lax.axis_index("dp"), lax.axis_index("tensor")
    width = q_ref.shape[1]
    chunk = cap * PBLK
    slots = peers * cap
    pairs = blocks // 2
    cand = neg * PBLK
    tiles = slots * PBLK // LANES
    want_at = 0
    slot_at = want_at + slots
    id_at = slot_at + blocks * neg
    ent_at = id_at + blocks * neg
    inv_at = ent_at + blocks * slots
    last = OWN - 1

    barrier = pltpu.get_barrier_semaphore()

    def greet(step, carry):
        pl.semaphore_signal(
            barrier, inc=1, device_id={"dp": lax.rem(me + step, peers)}, device_id_type=MESH
        )
        return carry

    lax.fori_loop(1, peers, greet, 0)
    for step in range(1, 4):
        pl.semaphore_signal(
            barrier, inc=1, device_id={"tensor": lax.rem(shard + step, 4)}, device_id_type=MESH
        )

    def pack(peer, target, offset):
        for k in range(cap):
            block = tab[want_at + peer * cap + k]
            target[pl.ds(offset + k * PBLK, PBLK), :] = p_ref[pl.ds(block * PBLK, PBLK), :]

    def chunk_rows(peer):
        return pl.ds(pl.multiple_of(peer * chunk, PBLK), chunk)

    def fetch(peer):
        return pltpu.make_async_remote_copy(
            src_ref=sendbuf.at[chunk_rows(peer)],
            dst_ref=panels.at[chunk_rows(me)],
            send_sem=send1.at[peer],
            recv_sem=recv1.at[me],
            device_id={"dp": peer},
            device_id_type=MESH,
        )

    def fetched(peer):
        return pltpu.make_async_remote_copy(
            src_ref=sendbuf.at[chunk_rows(me)],
            dst_ref=panels.at[chunk_rows(peer)],
            send_sem=send1.at[me],
            recv_sem=recv1.at[peer],
            device_id={"dp": peer},
            device_id_type=MESH,
        )

    pl.semaphore_wait(barrier, peers - 1 + 3)

    def start_fetch(step, carry):
        peer = partner(me, peers - step, peers)
        pack(peer, sendbuf, pl.multiple_of(peer * chunk, PBLK))
        fetch(peer).start()
        return carry

    lax.fori_loop(1, peers, start_fetch, 0)
    pack(me, panels, pl.multiple_of(me * chunk, PBLK))

    low_half = lax.broadcasted_iota(jnp.int32, (PBLK, LANES), 1) < QBLK
    low_row = lax.broadcasted_iota(jnp.int32, (1, LANES), 1) < QBLK

    def query_terms(j, carry):
        block = q_ref[pl.ds(pl.multiple_of(j * LANES, LANES), LANES), :].astype(F32)
        square = block * block

        def put(k, value):
            qsq[k, pl.ds(j, 1), :] = to_row(jnp.broadcast_to(value, (LANES, LANES)))

        prefix_squares(square, put)
        for e in range(neg):
            low = tab[id_at + (2 * j) * neg + e]
            high = tab[id_at + (2 * j + 1) * neg + e]
            cid[j, e * PBLK : (e + 1) * PBLK, :] = jnp.where(
                low_half, low, high
            ) * PBLK + lax.broadcasted_iota(jnp.int32, (PBLK, LANES), 0)
        return carry

    def prefix_squares(square, put):
        @pl.when(shard == 0)
        def _():
            first = square[:, :LANES]
            total = jnp.sum(jnp.where(low_row, first, 0.0), axis=1, keepdims=True)
            put(0, total)
            total = jnp.sum(first, axis=1, keepdims=True)
            put(1, total)
            for k in range(2, OWN):
                total = total + jnp.sum(
                    square[:, MINP * 2 ** (k - 1) : MINP * 2**k], axis=1, keepdims=True
                )
                put(k, total)

        @pl.when(shard != 0)
        def _():
            put(last, jnp.sum(square, axis=1, keepdims=True))

    lax.fori_loop(0, pairs, query_terms, 0)

    for k in range(OWN):
        half[k, :, cand : cand + PBLK, :] = jnp.zeros((pairs, PBLK, LANES), BF16)
        terms[k, :, cand : cand + PBLK, :] = jnp.zeros((pairs, PBLK, LANES), F32)
    back[...] = jnp.zeros_like(back)
    small[...] = jnp.zeros_like(small)

    def forward(step, carry):
        peer = partner(me, lax.rem(peers - step, peers), peers)

        @pl.when(step > 0)
        def _():
            fetched(peer).wait_recv()

        here = chunk_rows(peer)
        square = panels[here, :].astype(F32)
        square = square * square

        def put(k, value):
            psq[k, here, :] = jnp.broadcast_to(value, (chunk, LANES))

        prefix_squares(square, put)

        def keep(k, value):
            for j in range(pairs):
                dots[k, j, here, :] = value[:, j * LANES : (j + 1) * LANES]

        @pl.when(shard == 0)
        def _():
            first, query = panels[here, :LANES], q_ref[:, :LANES]
            keep(0, dot_nt(jnp.where(low_row, first, jnp.zeros((), BF16)), query))
            total = dot_nt(first, query)
            keep(1, total)
            for k in range(2, OWN):
                span = slice(MINP * 2 ** (k - 1), MINP * 2**k)
                total = total + dot_nt(panels[here, span], q_ref[:, span])
                keep(k, total)

        @pl.when(shard != 0)
        def _():
            keep(last, dot_nt(panels[here, :], q_ref[...]))

        if chunk == LANES:
            small[pl.ds(peer, 1), :] = to_row(psq[last, here, :])
        return carry

    lax.fori_loop(0, peers, forward, 0)

    def pick(ref, k, j, lead):
        parts = []
        for e in range(neg):
            low = tab[slot_at + (2 * j) * neg + e] * PBLK
            high = tab[slot_at + (2 * j + 1) * neg + e] * PBLK
            low = ref[lead(k, j) + (pl.ds(low, PBLK),)]
            high = ref[lead(k, j) + (pl.ds(high, PBLK),)]
            parts.append(jnp.where(low_half, low, high))
        return jnp.concatenate(parts, axis=0)

    def pick_dots(k, j):
        return pick(dots, k, j, lambda k, j: (k, j))

    def pick_squares(k, j):
        return pick(psq, k, j, lambda k, j: (k,))

    def small_copy(target, slot):
        return pltpu.make_async_remote_copy(
            src_ref=small, dst_ref=got_small.at[slot], send_sem=sm_send.at[0],
            recv_sem=sm_recv.at[slot], device_id={"tensor": target}, device_id_type=MESH,
        )

    def dots_copy(target, slot, j):
        return pltpu.make_async_remote_copy(
            src_ref=gathered.at[j], dst_ref=got.at[slot, j], send_sem=dg_send.at[j],
            recv_sem=dg_recv.at[slot, j], device_id={"tensor": target}, device_id_type=MESH,
        )

    def later_copy(j):
        return pltpu.make_async_remote_copy(
            src_ref=coef.at[last, j], dst_ref=got.at[0, j], send_sem=cf_send.at[0, j],
            recv_sem=dg_recv.at[0, j], device_id={"tensor": 0}, device_id_type=MESH,
        )

    def half_copy(target, j):
        return pltpu.make_async_remote_copy(
            src_ref=half.at[last, j, pl.ds(0, cand)], dst_ref=half.at[last, j, pl.ds(0, cand)],
            send_sem=cf_send.at[target - 1, j], recv_sem=cf_recv.at[j],
            device_id={"tensor": target}, device_id_type=MESH,
        )

    for t in range(tiles if chunk != LANES else 0):
        small[t : t + 1, :] = to_row(psq[last, t * LANES : (t + 1) * LANES, :])
    small[tiles : tiles + pairs, :] = qsq[last, 0:pairs, :]

    def widen():
        for t in range(tiles):
            psq[last, t * LANES : (t + 1) * LANES, :] = to_column(small[t : t + 1, :])
        qsq[last, 0:pairs, :] = small[tiles : tiles + pairs, :]

    def each_pair(body):
        def step(j, carry):
            body(j)
            return carry

        lax.fori_loop(0, pairs, step, 0)

    def prefix_terms(products, squares, k, j, weight):
        number = cid[j]
        live = number >= 0
        query_scale = lax.rsqrt(qsq[k, pl.ds(j, 1), :] + EPS)
        passage_scale = jnp.where(live, lax.rsqrt(squares + EPS), 0.0)
        scale = query_scale * passage_scale * INV_TEMP
        logits = products * scale
        exponent = jnp.where(live, jnp.exp(logits), 0.0)
        total = jnp.sum(exponent, axis=0, keepdims=True)
        hit = number == pos_ref[pl.ds(j, 1), :]
        loss = jnp.log(total) - jnp.sum(jnp.where(hit, logits, 0.0), axis=0, keepdims=True)
        gradient = weight * (exponent * (1.0 / total) - jnp.where(hit, 1.0, 0.0))
        inner = gradient * logits
        row = query_scale * query_scale * jnp.sum(inner, axis=0, keepdims=True)
        return gradient * scale, row, passage_scale * passage_scale * inner, weight * loss

    def one_prefix(products, j, weight):
        value, row, column, loss = prefix_terms(
            products, pick_squares(last, j), last, j, weight
        )
        coef[last, j] = value
        terms[last, j, 0:cand, :] = column
        rows[last, pl.ds(j, 1), :] = row
        back[pl.ds(tiles + pairs + j, 1), :] = loss

    def pick_half(ref, k, j, slot):
        low = tab[ent_at + (2 * j) * slots + slot] * PBLK
        high = tab[ent_at + (2 * j + 1) * slots + slot] * PBLK
        return jnp.where(
            low_half,
            ref[k, j, pl.ds(low, PBLK), :],
            ref[k, j, pl.ds(high, PBLK), :],
        )

    def column_sums(count):
        def step(slot, carry):
            for k in range(OWN - count, OWN):
                total = pick_half(terms, k, 0, slot)
                for j in range(1, pairs):
                    total = total + pick_half(terms, k, j, slot)
                cols[k, pl.ds(pl.multiple_of(slot * PBLK, PBLK), PBLK), :] = jnp.broadcast_to(
                    jnp.sum(total, axis=1, keepdims=True), (PBLK, LANES)
                )
            return carry

        lax.fori_loop(0, slots, step, 0)
        for t in range(tiles):
            back[t : t + 1, :] = to_row(cols[last, t * LANES : (t + 1) * LANES, :])
        back[tiles : tiles + pairs, :] = rows[last, 0:pairs, :]

    def back_copy(step, slot):
        return pltpu.make_async_remote_copy(
            src_ref=back, dst_ref=got_back.at[slot], send_sem=sb_send.at[step],
            recv_sem=sb_recv.at[slot], device_id={"tensor": lax.rem(shard + step, 4)},
            device_id_type=MESH,
        )

    def send_back():
        for step in range(1, 4):
            back_copy(step, shard).start()

    @pl.when(shard == 0)
    def _():
        small_copy(1, 0).start()

        def hand_on(j):
            gathered[j] = pick_dots(last, j)
            dots_copy(1, 0, j).start()

        each_pair(hand_on)

        def own(j):
            value = row = column = loss = None
            for k in reversed(range(OWN)):
                products = gathered[j] if k == last else pick_dots(k, j)
                part = prefix_terms(products, pick_squares(k, j), k, j, float(2**k))
                if k == last:
                    value, row, column, loss = part
                else:
                    value, row, column, loss = (
                        value + part[0], row + part[1], column + part[2], loss + part[3]
                    )
                coef[k, j] = value
                rows[k, pl.ds(j, 1), :] = row
                terms[k, j, 0:cand, :] = column
            back[pl.ds(tiles + pairs + j, 1), :] = loss

        each_pair(own)
        column_sums(OWN)
        send_back()

        def finish(j):
            later_copy(j).wait_recv()
            for k in range(OWN):
                half[k, j, 0:cand, :] = (coef[k, j] + got[0, j]).astype(BF16)

        each_pair(finish)
        small_copy(1, 0).wait_send()
        each_pair(lambda j: dots_copy(1, 0, j).wait_send())

    @pl.when(shard == 1)
    def _():
        small_copy(3, 0).wait_recv()
        small[...] = small[...] + got_small[0]
        small_copy(3, 0).start()

        def hand_on(j):
            dots_copy(3, 0, j).wait_recv()
            gathered[j] = pick_dots(last, j) + got[0, j]
            dots_copy(3, 0, j).start()

        each_pair(hand_on)
        widen()
        each_pair(lambda j: one_prefix(gathered[j], j, 32.0))
        column_sums(1)
        send_back()

        def finish(j):
            half_copy(1, j).wait_recv()
            total = coef[last, j] + half[last, j, 0:cand, :].astype(F32)
            coef[last, j] = total
            later_copy(j).start()
            half[last, j, 0:cand, :] = total.astype(BF16)

        each_pair(finish)
        small_copy(3, 0).wait_send()
        each_pair(lambda j: dots_copy(3, 0, j).wait_send())
        each_pair(lambda j: later_copy(j).wait_send())

    @pl.when(shard == 2)
    def _():
        small_copy(3, 1).start()

        def hand_on(j):
            gathered[j] = pick_dots(last, j)
            dots_copy(3, 1, j).start()

        each_pair(hand_on)
        cols[last] = jnp.zeros_like(cols[last])
        rows[last] = jnp.zeros_like(rows[last])
        send_back()
        each_pair(lambda j: half_copy(2, j).wait_recv())
        small_copy(3, 1).wait_send()
        each_pair(lambda j: dots_copy(3, 1, j).wait_send())

    @pl.when(shard == 3)
    def _():
        small_copy(2, 0).wait_recv()
        small_copy(2, 1).wait_recv()
        small[...] = small[...] + got_small[0] + got_small[1]
        widen()

        def answer(j):
            mine = pick_dots(last, j)
            dots_copy(2, 1, j).wait_recv()
            dots_copy(2, 0, j).wait_recv()
            one_prefix(mine + got[0, j] + got[1, j], j, 64.0)
            half[last, j, 0:cand, :] = coef[last, j].astype(BF16)
            half_copy(1, j).start()
            half_copy(2, j).start()

        each_pair(answer)
        column_sums(1)
        send_back()
        each_pair(lambda j: half_copy(1, j).wait_send())
        each_pair(lambda j: half_copy(2, j).wait_send())

    later = jnp.zeros(back.shape, F32)
    loss = back[tiles + pairs : tiles + 2 * pairs, :]
    for step in range(1, 4):
        other = lax.rem(shard + step, 4)
        back_copy(step, other).wait_recv()
        part = got_back[other]
        later = later + jnp.where(other > shard, 1.0, 0.0) * part
        loss = loss + part[tiles + pairs : tiles + 2 * pairs, :]
    weight_total = sum(2.0**k for k in range(NPRE))
    loss_ref[...] = loss / weight_total

    def add_later(count):
        for t in range(tiles):
            extra = to_column(later[t : t + 1, :])
            for k in range(OWN - count, OWN):
                cols[k, t * LANES : (t + 1) * LANES, :] += extra
        for k in range(OWN - count, OWN):
            rows[k, 0:pairs, :] += later[tiles : tiles + pairs, :]

    @pl.when(shard == 0)
    def _():
        add_later(OWN)

    @pl.when(shard != 0)
    def _():
        add_later(1)

    spans = [(k, slice(MINP * 2 ** (k - 1), MINP * 2**k)) for k in range(2, OWN)]

    def build(k, peer):
        def step(i, carry):
            slot = peer * cap + i
            for j in range(pairs):
                grid[
                    k, pl.ds(pl.multiple_of(slot * PBLK, PBLK), PBLK), j * LANES : (j + 1) * LANES
                ] = pick_half(half, k, j, slot)
            return carry

        lax.fori_loop(0, cap, step, 0)

    def send_grad(peer):
        return pltpu.make_async_remote_copy(
            src_ref=gradbuf.at[chunk_rows(peer)], dst_ref=returned.at[me, pl.ds(0, chunk)],
            send_sem=send2.at[peer], recv_sem=recv2.at[me],
            device_id={"dp": peer}, device_id_type=MESH,
        )

    def came_back(peer):
        return pltpu.make_async_remote_copy(
            src_ref=gradbuf.at[chunk_rows(me)], dst_ref=returned.at[peer, pl.ds(0, chunk)],
            send_sem=send2.at[me], recv_sem=recv2.at[peer],
            device_id={"dp": peer}, device_id_type=MESH,
        )

    def passage_part(step, carry):
        peer = partner(me, peers - step, peers)
        here = chunk_rows(peer)

        def put(span, k, product):
            piece = product - cols[k, here, 0:1] * panels[here, span].astype(F32)
            gradbuf[here, span] = piece.astype(BF16)

        @pl.when(shard == 0)
        def _():
            for k in range(OWN):
                build(k, peer)
            query = q_ref[:, :LANES]
            first = panels[here, :LANES].astype(F32)
            low = jnp.dot(grid[0, here, :], query, preferred_element_type=F32)
            low = low - cols[0, here, :] * first
            high = jnp.dot(grid[1, here, :], query, preferred_element_type=F32)
            high = high - cols[1, here, :] * first
            gradbuf[here, :LANES] = jnp.where(low_row, low, high).astype(BF16)
            for k, span in spans:
                put(span, k, jnp.dot(grid[k, here, :], q_ref[:, span], preferred_element_type=F32))

        @pl.when(shard != 0)
        def _():
            build(last, peer)
            put(
                slice(0, width), last,
                jnp.dot(grid[last, here, :], q_ref[...], preferred_element_type=F32),
            )

        @pl.when(step < peers)
        def _():
            send_grad(peer).start()

        @pl.when(step == peers)
        def _():
            returned[me, 0:chunk, :] = gradbuf[here, :]

        return carry

    lax.fori_loop(1, peers + 1, passage_part, 0)

    def query_part(j, carry):
        here = pl.ds(pl.multiple_of(j * LANES, LANES), LANES)

        def column(k):
            return to_column(rows[k, pl.ds(j, 1), :])

        def product(k, span):
            return dot_tn(grid[k, :, here], panels[:, span])

        @pl.when(shard == 0)
        def _():
            query = q_ref[here, :LANES].astype(F32)
            first = slice(0, LANES)
            low = product(0, first) - column(0) * query
            high = product(1, first) - column(1) * query
            dq_ref[here, :LANES] = jnp.where(low_row, low, high).astype(BF16)
            for k, span in spans:
                piece = product(k, span) - column(k)[:, 0:1] * q_ref[here, span].astype(F32)
                dq_ref[here, span] = piece.astype(BF16)

        @pl.when(shard != 0)
        def _():
            piece = product(last, slice(0, width)) - column(last)[:, 0:1] * q_ref[here, :].astype(F32)
            dq_ref[here, :] = piece.astype(BF16)

        return carry

    lax.fori_loop(0, pairs, query_part, 0)

    returned[:, chunk : chunk + PBLK, :] = jnp.zeros((peers, PBLK, width), BF16)

    def drain(step, carry):
        peer = lax.rem(me + step, peers)
        came_back(peer).wait_recv()
        return carry

    lax.fori_loop(1, peers, drain, 0)

    def total_block(block, carry):
        def add(peer, total):
            row = tab[inv_at + peer * local_blocks + block] * PBLK
            return total + returned[peer, pl.ds(row, PBLK), :].astype(F32)

        total = lax.fori_loop(0, peers, add, jnp.zeros((PBLK, width), F32))
        dp_ref[pl.ds(pl.multiple_of(block * PBLK, PBLK), PBLK), :] = total.astype(BF16)
        return carry

    lax.fori_loop(0, local_blocks, total_block, 0)

    def sent(step, carry):
        peer = lax.rem(me + step, peers)
        fetch(peer).wait_send()
        send_grad(peer).wait_send()
        return carry

    lax.fori_loop(1, peers, sent, 0)
    for step in range(1, 4):
        back_copy(step, shard).wait_send()


def per_device(queries, passages, neg_lists, positives):
    peer_count = lax.axis_size("dp")
    width = queries.shape[1]
    blocks_here = neg_lists.shape[0] // peer_count
    neg_count = neg_lists.shape[1]
    local_blocks = passages.shape[0] // PBLK
    capacity = blocks_here * neg_count // 2 // peer_count
    slot_count = peer_count * capacity
    cand = neg_count * PBLK
    pairs = blocks_here // 2
    my_index = lax.axis_index("dp")
    flat_all = neg_lists.reshape(peer_count, blocks_here * neg_count)
    is_first, home_slot, entry_slot, local_block = jax.vmap(
        partial(request_plan, capacity=capacity, per_owner=local_blocks)
    )(flat_all)
    targets = my_index * capacity + jnp.arange(capacity, dtype=jnp.int32)
    target_hit = is_first[:, :, None] & (home_slot[:, :, None] == targets[None, None, :])
    wanted = jnp.sum(jnp.where(target_hit, local_block[:, :, None] + 1, 0), axis=1) - 1
    own_ids = lax.dynamic_index_in_dim(flat_all, my_index, 0, keepdims=False)
    own_slot = lax.dynamic_index_in_dim(entry_slot, my_index, 0, keepdims=False)
    own_live = own_ids >= 0
    entries = jnp.arange(neg_count, dtype=jnp.int32)[None, :, None]
    at_slot = (
        own_slot.reshape(blocks_here, neg_count, 1) == jnp.arange(slot_count, dtype=jnp.int32)
    ) & own_live.reshape(blocks_here, neg_count, 1)
    entry_of = neg_count + jnp.sum(jnp.where(at_slot, entries - neg_count, 0), axis=1)
    named = wanted[:, :, None] == jnp.arange(local_blocks, dtype=jnp.int32)
    ranks = jnp.arange(capacity, dtype=jnp.int32)[None, :, None]
    rank_of = capacity + jnp.sum(jnp.where(named, ranks - capacity, 0), axis=1)
    table = jnp.concatenate([
        jnp.maximum(wanted, 0).reshape(-1),
        jnp.where(own_live, own_slot, 0),
        jnp.where(own_live, own_ids, -1),
        entry_of.reshape(-1),
        rank_of.reshape(-1),
    ]).astype(jnp.int32)

    slot_rows = slot_count * PBLK
    query_count = queries.shape[0]
    smalls = slot_rows // LANES + 2 * pairs
    vmem, dma = pltpu.VMEM, pltpu.SemaphoreType.DMA
    whole = pl.BlockSpec(memory_space=pltpu.VMEM)
    query_grad, passage_grad, loss = pl.pallas_call(
        partial(kernel, peer_count, capacity, blocks_here, neg_count, local_blocks),
        out_shape=(
            jax.ShapeDtypeStruct(queries.shape, BF16),
            jax.ShapeDtypeStruct(passages.shape, BF16),
            jax.ShapeDtypeStruct((pairs, LANES), F32),
        ),
        in_specs=[pl.BlockSpec(memory_space=pltpu.SMEM), whole, whole, whole],
        out_specs=(whole, whole, whole),
        scratch_shapes=[
            vmem((slot_rows, width), BF16),
            vmem((slot_rows, width), BF16),
            vmem((slot_rows, width), BF16),
            vmem((peer_count, (capacity + 1) * PBLK, width), BF16),
            vmem((OWN, pairs, slot_rows, LANES), F32),
            vmem((OWN, slot_rows, LANES), F32),
            vmem((pairs, cand, LANES), jnp.int32),
            vmem((pairs, cand, LANES), F32),
            vmem((2, pairs, cand, LANES), F32),
            vmem((OWN, pairs, cand, LANES), F32),
            vmem((OWN, pairs, cand + PBLK, LANES), F32),
            vmem((OWN, pairs, cand + PBLK, LANES), BF16),
            vmem((OWN, slot_rows, query_count), BF16),
            vmem((OWN, slot_rows, LANES), F32),
            vmem((OWN, 8, LANES), F32),
            vmem((OWN, 8, LANES), F32),
            vmem((smalls, LANES), F32),
            vmem((2, smalls, LANES), F32),
            vmem((smalls, LANES), F32),
            vmem((4, smalls, LANES), F32),
            dma((peer_count,)), dma((peer_count,)), dma((peer_count,)), dma((peer_count,)),
            dma((pairs,)), dma((2, pairs)), dma((1,)), dma((2,)),
            dma((2, pairs)), dma((pairs,)), dma((4,)), dma((4,)),
        ],
        compiler_params=pltpu.CompilerParams(
            collective_id=0, has_side_effects=True, vmem_limit_bytes=56 * 2**20
        ),
        name="matryoshka",
    )(table, positives.reshape(pairs, LANES), queries, passages)
    return query_grad, passage_grad, loss.reshape(query_count)


def solution(mesh):
    return jax.shard_map(
        per_device,
        mesh=mesh,
        in_specs=(P("dp", "tensor"), P("dp", "tensor"), P(), P("dp")),
        out_specs=(P("dp", "tensor"), P("dp", "tensor"), P("dp")),
        check_vma=False,
    )
```

```python
from functools import partial

import jax
import jax.numpy as jnp
from jax import lax
from jax.experimental import pallas as pl
from jax.experimental.pallas import tpu as pltpu
from jax.sharding import PartitionSpec as P

MINP = 64
NPRE = 7
PBLK = 16
QBLK = 64
LANES = 128
OWN = 5

EPS = 1e-06
INV_TEMP = 20.0
MESH = pl.DeviceIdType.MESH
F32 = jnp.float32
BF16 = jnp.bfloat16


def request_plan(flat_ids, capacity, per_owner):
    entry_count = flat_ids.shape[0]
    is_valid = flat_ids >= 0
    entry_order = jnp.arange(entry_count, dtype=jnp.int32)
    earlier = entry_order[None, :] < entry_order[:, None]
    same_block = (flat_ids[:, None] == flat_ids[None, :]) & is_valid[None, :]
    is_first = is_valid & jnp.logical_not(jnp.any(same_block & earlier, axis=1))
    owner_index = jnp.where(is_valid, flat_ids // per_owner, 0)
    local_block = jnp.where(is_valid, flat_ids % per_owner, 0)
    owner_rank = jnp.sum(
        ((owner_index[:, None] == owner_index[None, :]) & earlier & is_first[None, :]).astype(
            jnp.int32
        ),
        axis=1,
    )
    home_slot = jnp.where(is_first, owner_index * capacity + owner_rank, 0)
    entry_slot = jnp.sum(jnp.where(same_block & is_first[None, :], home_slot[None, :], 0), axis=1)
    return (is_first, home_slot, entry_slot, local_block)


def dot_nt(left, right):
    return lax.dot_general(left, right, (((1,), (1,)), ((), ())), preferred_element_type=F32)


def dot_tn(left, right):
    return lax.dot_general(left, right, (((0,), (0,)), ((), ())), preferred_element_type=F32)


def partner(me, step, peers):
    other, digit = 0, 1
    while digit < peers:
        other = other + lax.rem(lax.div(me, digit) + lax.div(step, digit), 2) * digit
        digit *= 2
    return other


def to_row(column):
    return column.T[0:1, :]


def to_column(row):
    return jnp.broadcast_to(row, (LANES, LANES)).T


def kernel(
    peers, cap, blocks, neg, local_blocks,
    tab, pos_ref, q_ref, p_ref, dq_ref, dp_ref, loss_ref,
    panels, sendbuf, gradbuf, near, far, total_grad, dots, psq, cid, gathered, got, coef, terms, half,
    grid, cols, qsq, rows, small, got_small, back, got_back,
    send1, recv1, send2, recv2, dg_send, dg_recv, sm_send, sm_recv, cf_send, cf_recv,
    sb_send, sb_recv,
):
    me, shard = lax.axis_index("dp"), lax.axis_index("tensor")
    width = q_ref.shape[1]
    chunk = cap * PBLK
    slots = peers * cap
    pairs = blocks // 2
    cand = neg * PBLK
    tiles = slots * PBLK // LANES
    want_at = 0
    slot_at = want_at + slots
    id_at = slot_at + blocks * neg
    ent_at = id_at + blocks * neg
    inv_at = ent_at + blocks * slots
    last = OWN - 1

    barrier = pltpu.get_barrier_semaphore()

    def greet(step, carry):
        pl.semaphore_signal(
            barrier, inc=1, device_id={"dp": lax.rem(me + step, peers)}, device_id_type=MESH
        )
        return carry

    lax.fori_loop(1, peers, greet, 0)
    for step in range(1, 4):
        pl.semaphore_signal(
            barrier, inc=1, device_id={"tensor": lax.rem(shard + step, 4)}, device_id_type=MESH
        )

    def pack(peer, target, offset):
        for k in range(cap):
            block = tab[want_at + peer * cap + k]
            target[pl.ds(offset + k * PBLK, PBLK), :] = p_ref[pl.ds(block * PBLK, PBLK), :]

    def chunk_rows(peer):
        return pl.ds(pl.multiple_of(peer * chunk, PBLK), chunk)

    def fetch(peer):
        return pltpu.make_async_remote_copy(
            src_ref=sendbuf.at[chunk_rows(peer)],
            dst_ref=panels.at[chunk_rows(me)],
            send_sem=send1.at[peer],
            recv_sem=recv1.at[me],
            device_id={"dp": peer},
            device_id_type=MESH,
        )

    def fetched(peer):
        return pltpu.make_async_remote_copy(
            src_ref=sendbuf.at[chunk_rows(me)],
            dst_ref=panels.at[chunk_rows(peer)],
            send_sem=send1.at[me],
            recv_sem=recv1.at[peer],
            device_id={"dp": peer},
            device_id_type=MESH,
        )

    pl.semaphore_wait(barrier, peers - 1 + 3)

    def start_fetch(step, carry):
        peer = partner(me, peers - step, peers)
        pack(peer, sendbuf, pl.multiple_of(peer * chunk, PBLK))
        fetch(peer).start()
        return carry

    lax.fori_loop(1, peers, start_fetch, 0)
    pack(me, panels, pl.multiple_of(me * chunk, PBLK))

    low_half = lax.broadcasted_iota(jnp.int32, (PBLK, LANES), 1) < QBLK
    low_row = lax.broadcasted_iota(jnp.int32, (1, LANES), 1) < QBLK

    def query_terms(j, carry):
        block = q_ref[pl.ds(pl.multiple_of(j * LANES, LANES), LANES), :].astype(F32)
        square = block * block

        def put(k, value):
            qsq[k, pl.ds(j, 1), :] = to_row(jnp.broadcast_to(value, (LANES, LANES)))

        prefix_squares(square, put)
        for e in range(neg):
            low = tab[id_at + (2 * j) * neg + e]
            high = tab[id_at + (2 * j + 1) * neg + e]
            cid[j, e * PBLK : (e + 1) * PBLK, :] = jnp.where(
                low_half, low, high
            ) * PBLK + lax.broadcasted_iota(jnp.int32, (PBLK, LANES), 0)
        return carry

    def prefix_squares(square, put):
        @pl.when(shard == 0)
        def _():
            first = square[:, :LANES]
            total = jnp.sum(jnp.where(low_row, first, 0.0), axis=1, keepdims=True)
            put(0, total)
            total = jnp.sum(first, axis=1, keepdims=True)
            put(1, total)
            for k in range(2, OWN):
                total = total + jnp.sum(
                    square[:, MINP * 2 ** (k - 1) : MINP * 2**k], axis=1, keepdims=True
                )
                put(k, total)

        @pl.when(shard != 0)
        def _():
            put(last, jnp.sum(square, axis=1, keepdims=True))

    lax.fori_loop(0, pairs, query_terms, 0)

    for k in range(OWN):
        half[k, :, cand : cand + PBLK, :] = jnp.zeros((pairs, PBLK, LANES), BF16)
        terms[k, :, cand : cand + PBLK, :] = jnp.zeros((pairs, PBLK, LANES), F32)
    back[...] = jnp.zeros_like(back)
    small[...] = jnp.zeros_like(small)

    def forward(step, carry):
        peer = partner(me, lax.rem(peers - step, peers), peers)

        @pl.when(step > 0)
        def _():
            fetched(peer).wait_recv()

        here = chunk_rows(peer)
        square = panels[here, :].astype(F32)
        square = square * square

        def put(k, value):
            psq[k, here, :] = jnp.broadcast_to(value, (chunk, LANES))

        prefix_squares(square, put)

        def keep(k, value):
            for j in range(pairs):
                dots[k, j, here, :] = value[:, j * LANES : (j + 1) * LANES]

        @pl.when(shard == 0)
        def _():
            first, query = panels[here, :LANES], q_ref[:, :LANES]
            keep(0, dot_nt(jnp.where(low_row, first, jnp.zeros((), BF16)), query))
            total = dot_nt(first, query)
            keep(1, total)
            for k in range(2, OWN):
                span = slice(MINP * 2 ** (k - 1), MINP * 2**k)
                total = total + dot_nt(panels[here, span], q_ref[:, span])
                keep(k, total)

        @pl.when(shard != 0)
        def _():
            keep(last, dot_nt(panels[here, :], q_ref[...]))

        if chunk == LANES:
            small[pl.ds(peer, 1), :] = to_row(psq[last, here, :])
        return carry

    lax.fori_loop(0, peers, forward, 0)

    def pick(ref, k, j, lead):
        parts = []
        for e in range(neg):
            low = tab[slot_at + (2 * j) * neg + e] * PBLK
            high = tab[slot_at + (2 * j + 1) * neg + e] * PBLK
            low = ref[lead(k, j) + (pl.ds(low, PBLK),)]
            high = ref[lead(k, j) + (pl.ds(high, PBLK),)]
            parts.append(jnp.where(low_half, low, high))
        return jnp.concatenate(parts, axis=0)

    def pick_dots(k, j):
        return pick(dots, k, j, lambda k, j: (k, j))

    def pick_squares(k, j):
        return pick(psq, k, j, lambda k, j: (k,))

    def small_copy(target, slot):
        return pltpu.make_async_remote_copy(
            src_ref=small, dst_ref=got_small.at[slot], send_sem=sm_send.at[0],
            recv_sem=sm_recv.at[slot], device_id={"tensor": target}, device_id_type=MESH,
        )

    def dots_copy(target, slot, j):
        return pltpu.make_async_remote_copy(
            src_ref=gathered.at[j], dst_ref=got.at[slot, j], send_sem=dg_send.at[j],
            recv_sem=dg_recv.at[slot, j], device_id={"tensor": target}, device_id_type=MESH,
        )

    def later_copy(j):
        return pltpu.make_async_remote_copy(
            src_ref=coef.at[last, j], dst_ref=got.at[0, j], send_sem=cf_send.at[0, j],
            recv_sem=dg_recv.at[0, j], device_id={"tensor": 0}, device_id_type=MESH,
        )

    def half_copy(target, j):
        return pltpu.make_async_remote_copy(
            src_ref=half.at[last, j, pl.ds(0, cand)], dst_ref=half.at[last, j, pl.ds(0, cand)],
            send_sem=cf_send.at[target - 1, j], recv_sem=cf_recv.at[j],
            device_id={"tensor": target}, device_id_type=MESH,
        )

    for t in range(tiles if chunk != LANES else 0):
        small[t : t + 1, :] = to_row(psq[last, t * LANES : (t + 1) * LANES, :])
    small[tiles : tiles + pairs, :] = qsq[last, 0:pairs, :]

    def widen():
        for t in range(tiles):
            psq[last, t * LANES : (t + 1) * LANES, :] = to_column(small[t : t + 1, :])
        qsq[last, 0:pairs, :] = small[tiles : tiles + pairs, :]

    def each_pair(body):
        def step(j, carry):
            body(j)
            return carry

        lax.fori_loop(0, pairs, step, 0)

    def prefix_terms(products, squares, k, j, weight):
        number = cid[j]
        live = number >= 0
        query_scale = lax.rsqrt(qsq[k, pl.ds(j, 1), :] + EPS)
        passage_scale = jnp.where(live, lax.rsqrt(squares + EPS), 0.0)
        scale = query_scale * passage_scale * INV_TEMP
        logits = products * scale
        exponent = jnp.where(live, jnp.exp(logits), 0.0)
        total = jnp.sum(exponent, axis=0, keepdims=True)
        hit = number == pos_ref[pl.ds(j, 1), :]
        loss = jnp.log(total) - jnp.sum(jnp.where(hit, logits, 0.0), axis=0, keepdims=True)
        gradient = weight * (exponent * (1.0 / total) - jnp.where(hit, 1.0, 0.0))
        inner = gradient * logits
        row = query_scale * query_scale * jnp.sum(inner, axis=0, keepdims=True)
        return gradient * scale, row, passage_scale * passage_scale * inner, weight * loss

    def one_prefix(products, j, weight):
        value, row, column, loss = prefix_terms(
            products, pick_squares(last, j), last, j, weight
        )
        coef[last, j] = value
        terms[last, j, 0:cand, :] = column
        rows[last, pl.ds(j, 1), :] = row
        back[pl.ds(tiles + pairs + j, 1), :] = loss

    def pick_half(ref, k, j, slot):
        low = tab[ent_at + (2 * j) * slots + slot] * PBLK
        high = tab[ent_at + (2 * j + 1) * slots + slot] * PBLK
        return jnp.where(
            low_half,
            ref[k, j, pl.ds(low, PBLK), :],
            ref[k, j, pl.ds(high, PBLK), :],
        )

    def column_sums(count):
        def step(slot, carry):
            for k in range(OWN - count, OWN):
                total = pick_half(terms, k, 0, slot)
                for j in range(1, pairs):
                    total = total + pick_half(terms, k, j, slot)
                cols[k, pl.ds(pl.multiple_of(slot * PBLK, PBLK), PBLK), :] = jnp.broadcast_to(
                    jnp.sum(total, axis=1, keepdims=True), (PBLK, LANES)
                )
            return carry

        lax.fori_loop(0, slots, step, 0)
        for t in range(tiles):
            back[t : t + 1, :] = to_row(cols[last, t * LANES : (t + 1) * LANES, :])
        back[tiles : tiles + pairs, :] = rows[last, 0:pairs, :]

    def back_copy(step, slot):
        return pltpu.make_async_remote_copy(
            src_ref=back, dst_ref=got_back.at[slot], send_sem=sb_send.at[step],
            recv_sem=sb_recv.at[slot], device_id={"tensor": lax.rem(shard + step, 4)},
            device_id_type=MESH,
        )

    def send_back():
        for step in range(1, 4):
            back_copy(step, shard).start()

    @pl.when(shard == 0)
    def _():
        small_copy(1, 0).start()

        def hand_on(j):
            gathered[j] = pick_dots(last, j)
            dots_copy(1, 0, j).start()

        each_pair(hand_on)

        def own(j):
            value = row = column = loss = None
            for k in reversed(range(OWN)):
                products = gathered[j] if k == last else pick_dots(k, j)
                part = prefix_terms(products, pick_squares(k, j), k, j, float(2**k))
                if k == last:
                    value, row, column, loss = part
                else:
                    value, row, column, loss = (
                        value + part[0], row + part[1], column + part[2], loss + part[3]
                    )
                coef[k, j] = value
                rows[k, pl.ds(j, 1), :] = row
                terms[k, j, 0:cand, :] = column
            back[pl.ds(tiles + pairs + j, 1), :] = loss

        each_pair(own)
        column_sums(OWN)
        send_back()

        def finish(j):
            later_copy(j).wait_recv()
            for k in range(OWN):
                half[k, j, 0:cand, :] = (coef[k, j] + got[0, j]).astype(BF16)

        each_pair(finish)
        small_copy(1, 0).wait_send()
        each_pair(lambda j: dots_copy(1, 0, j).wait_send())

    @pl.when(shard == 1)
    def _():
        small_copy(3, 0).wait_recv()
        small[...] = small[...] + got_small[0]
        small_copy(3, 0).start()

        def hand_on(j):
            dots_copy(3, 0, j).wait_recv()
            gathered[j] = pick_dots(last, j) + got[0, j]
            dots_copy(3, 0, j).start()

        each_pair(hand_on)
        widen()
        each_pair(lambda j: one_prefix(gathered[j], j, 32.0))
        column_sums(1)
        send_back()

        def finish(j):
            half_copy(1, j).wait_recv()
            total = coef[last, j] + half[last, j, 0:cand, :].astype(F32)
            coef[last, j] = total
            later_copy(j).start()
            half[last, j, 0:cand, :] = total.astype(BF16)

        each_pair(finish)
        small_copy(3, 0).wait_send()
        each_pair(lambda j: dots_copy(3, 0, j).wait_send())
        each_pair(lambda j: later_copy(j).wait_send())

    @pl.when(shard == 2)
    def _():
        small_copy(3, 1).start()

        def hand_on(j):
            gathered[j] = pick_dots(last, j)
            dots_copy(3, 1, j).start()

        each_pair(hand_on)
        cols[last] = jnp.zeros_like(cols[last])
        rows[last] = jnp.zeros_like(rows[last])
        send_back()
        each_pair(lambda j: half_copy(2, j).wait_recv())
        small_copy(3, 1).wait_send()
        each_pair(lambda j: dots_copy(3, 1, j).wait_send())

    @pl.when(shard == 3)
    def _():
        small_copy(2, 0).wait_recv()
        small_copy(2, 1).wait_recv()
        small[...] = small[...] + got_small[0] + got_small[1]
        widen()

        def answer(j):
            mine = pick_dots(last, j)
            dots_copy(2, 1, j).wait_recv()
            dots_copy(2, 0, j).wait_recv()
            one_prefix(mine + got[0, j] + got[1, j], j, 64.0)
            half[last, j, 0:cand, :] = coef[last, j].astype(BF16)
            half_copy(1, j).start()
            half_copy(2, j).start()

        each_pair(answer)
        column_sums(1)
        send_back()
        each_pair(lambda j: half_copy(1, j).wait_send())
        each_pair(lambda j: half_copy(2, j).wait_send())

    later = jnp.zeros(back.shape, F32)
    loss = back[tiles + pairs : tiles + 2 * pairs, :]
    for step in range(1, 4):
        other = lax.rem(shard + step, 4)
        back_copy(step, other).wait_recv()
        part = got_back[other]
        later = later + jnp.where(other > shard, 1.0, 0.0) * part
        loss = loss + part[tiles + pairs : tiles + 2 * pairs, :]
    weight_total = sum(2.0**k for k in range(NPRE))
    loss_ref[...] = loss / weight_total

    def add_later(count):
        for t in range(tiles):
            extra = to_column(later[t : t + 1, :])
            for k in range(OWN - count, OWN):
                cols[k, t * LANES : (t + 1) * LANES, :] += extra
        for k in range(OWN - count, OWN):
            rows[k, 0:pairs, :] += later[tiles : tiles + pairs, :]

    @pl.when(shard == 0)
    def _():
        add_later(OWN)

    @pl.when(shard != 0)
    def _():
        add_later(1)

    spans = [(k, slice(MINP * 2 ** (k - 1), MINP * 2**k)) for k in range(2, OWN)]

    def build(k, peer):
        def step(i, carry):
            slot = peer * cap + i
            for j in range(pairs):
                grid[
                    k, pl.ds(pl.multiple_of(slot * PBLK, PBLK), PBLK), j * LANES : (j + 1) * LANES
                ] = pick_half(half, k, j, slot)
            return carry

        lax.fori_loop(0, cap, step, 0)

    split = peers // 2

    def landing(step, is_far):
        return far.at[step - split] if is_far else near.at[step]

    def grad_copy(step, is_far):
        peer = partner(me, step, peers)
        return pltpu.make_async_remote_copy(
            src_ref=gradbuf.at[chunk_rows(peer)],
            dst_ref=landing(step, is_far).at[pl.ds(0, chunk)],
            send_sem=send2.at[step], recv_sem=recv2.at[step],
            device_id={"dp": peer}, device_id_type=MESH,
        )

    def passage_part(step):
        peer = partner(me, step, peers)
        here = chunk_rows(peer)

        def put(span, k, product):
            piece = product - cols[k, here, 0:1] * panels[here, span].astype(F32)
            gradbuf[here, span] = piece.astype(BF16)

        @pl.when(shard == 0)
        def _():
            for k in range(OWN):
                build(k, peer)
            query = q_ref[:, :LANES]
            first = panels[here, :LANES].astype(F32)
            low = jnp.dot(grid[0, here, :], query, preferred_element_type=F32)
            low = low - cols[0, here, :] * first
            high = jnp.dot(grid[1, here, :], query, preferred_element_type=F32)
            high = high - cols[1, here, :] * first
            gradbuf[here, :LANES] = jnp.where(low_row, low, high).astype(BF16)
            for k, span in spans:
                put(span, k, jnp.dot(grid[k, here, :], q_ref[:, span], preferred_element_type=F32))

        @pl.when(shard != 0)
        def _():
            build(last, peer)
            put(
                slice(0, width), last,
                jnp.dot(grid[last, here, :], q_ref[...], preferred_element_type=F32),
            )

    def far_part(i, carry):
        passage_part(peers - 1 - i)
        grad_copy(peers - 1 - i, True).start()
        return carry

    def near_part(i, carry):
        passage_part(split - i)
        grad_copy(split - i, False).start()
        return carry

    lax.fori_loop(0, split, far_part, 0)
    lax.fori_loop(1, split, near_part, 0)
    passage_part(0)
    near[0, 0:chunk, :] = gradbuf[chunk_rows(me), :]

    def query_part(j, carry):
        here = pl.ds(pl.multiple_of(j * LANES, LANES), LANES)

        def column(k):
            return to_column(rows[k, pl.ds(j, 1), :])

        def product(k, span):
            return dot_tn(grid[k, :, here], panels[:, span])

        @pl.when(shard == 0)
        def _():
            query = q_ref[here, :LANES].astype(F32)
            first = slice(0, LANES)
            low = product(0, first) - column(0) * query
            high = product(1, first) - column(1) * query
            dq_ref[here, :LANES] = jnp.where(low_row, low, high).astype(BF16)
            for k, span in spans:
                piece = product(k, span) - column(k)[:, 0:1] * q_ref[here, span].astype(F32)
                dq_ref[here, span] = piece.astype(BF16)

        @pl.when(shard != 0)
        def _():
            piece = product(last, slice(0, width)) - column(last)[:, 0:1] * q_ref[here, :].astype(F32)
            dq_ref[here, :] = piece.astype(BF16)

        return carry

    lax.fori_loop(0, pairs, query_part, 0)

    zeros = jnp.zeros((split, PBLK, width), BF16)
    near[:, chunk : chunk + PBLK, :] = zeros
    far[:, chunk : chunk + PBLK, :] = zeros

    def add_up(ref, first, block, total):
        def add(i, total):
            peer = partner(me, first + i, peers)
            row = tab[inv_at + peer * local_blocks + block] * PBLK
            return total + ref[i, pl.ds(row, PBLK), :].astype(F32)

        return lax.fori_loop(0, split, add, total)

    def block_rows(block):
        return pl.ds(pl.multiple_of(block * PBLK, PBLK), PBLK)

    def drain_near(step, carry):
        grad_copy(step, False).wait_recv()
        return carry

    def near_block(block, carry):
        total_grad[block_rows(block), :] = add_up(near, 0, block, jnp.zeros((PBLK, width), F32))
        return carry

    def drain_far(i, carry):
        grad_copy(split + i, True).wait_recv()
        return carry

    def far_block(block, carry):
        total = add_up(far, split, block, total_grad[block_rows(block), :])
        dp_ref[block_rows(block), :] = total.astype(BF16)
        return carry

    lax.fori_loop(1, split, drain_near, 0)
    lax.fori_loop(0, local_blocks, near_block, 0)
    lax.fori_loop(0, split, drain_far, 0)
    lax.fori_loop(0, local_blocks, far_block, 0)

    def sent(step, carry):
        fetch(partner(me, step, peers)).wait_send()
        return carry

    def near_sent(step, carry):
        grad_copy(step, False).wait_send()
        return carry

    def far_sent(i, carry):
        grad_copy(split + i, True).wait_send()
        return carry

    lax.fori_loop(1, peers, sent, 0)
    lax.fori_loop(1, split, near_sent, 0)
    lax.fori_loop(0, split, far_sent, 0)
    for step in range(1, 4):
        back_copy(step, shard).wait_send()


def copy_out(*refs):
    sources, targets, done = refs[:3], refs[3:6], refs[6]
    copies = [
        pltpu.make_async_copy(source, target, done.at[i])
        for i, (source, target) in enumerate(zip(sources, targets))
    ]
    for copy in copies:
        copy.start()
    for copy in copies:
        copy.wait()


def per_device(queries, passages, neg_lists, positives):
    peer_count = lax.axis_size("dp")
    width = queries.shape[1]
    blocks_here = neg_lists.shape[0] // peer_count
    neg_count = neg_lists.shape[1]
    local_blocks = passages.shape[0] // PBLK
    capacity = blocks_here * neg_count // 2 // peer_count
    slot_count = peer_count * capacity
    cand = neg_count * PBLK
    pairs = blocks_here // 2
    my_index = lax.axis_index("dp")
    flat_all = neg_lists.reshape(peer_count, blocks_here * neg_count)
    is_first, home_slot, entry_slot, local_block = jax.vmap(
        partial(request_plan, capacity=capacity, per_owner=local_blocks)
    )(flat_all)
    targets = my_index * capacity + jnp.arange(capacity, dtype=jnp.int32)
    target_hit = is_first[:, :, None] & (home_slot[:, :, None] == targets[None, None, :])
    wanted = jnp.sum(jnp.where(target_hit, local_block[:, :, None] + 1, 0), axis=1) - 1
    own_ids = lax.dynamic_index_in_dim(flat_all, my_index, 0, keepdims=False)
    own_slot = lax.dynamic_index_in_dim(entry_slot, my_index, 0, keepdims=False)
    own_live = own_ids >= 0
    entries = jnp.arange(neg_count, dtype=jnp.int32)[None, :, None]
    at_slot = (
        own_slot.reshape(blocks_here, neg_count, 1) == jnp.arange(slot_count, dtype=jnp.int32)
    ) & own_live.reshape(blocks_here, neg_count, 1)
    entry_of = neg_count + jnp.sum(jnp.where(at_slot, entries - neg_count, 0), axis=1)
    named = wanted[:, :, None] == jnp.arange(local_blocks, dtype=jnp.int32)
    ranks = jnp.arange(capacity, dtype=jnp.int32)[None, :, None]
    rank_of = capacity + jnp.sum(jnp.where(named, ranks - capacity, 0), axis=1)
    table = jnp.concatenate([
        jnp.maximum(wanted, 0).reshape(-1),
        jnp.where(own_live, own_slot, 0),
        jnp.where(own_live, own_ids, -1),
        entry_of.reshape(-1),
        rank_of.reshape(-1),
    ]).astype(jnp.int32)

    slot_rows = slot_count * PBLK
    query_count = queries.shape[0]
    smalls = slot_rows // LANES + 2 * pairs
    vmem, dma = pltpu.VMEM, pltpu.SemaphoreType.DMA
    whole = pl.BlockSpec(memory_space=pltpu.VMEM)
    query_grad, passage_grad, loss = pl.pallas_call(
        partial(kernel, peer_count, capacity, blocks_here, neg_count, local_blocks),
        out_shape=(
            jax.ShapeDtypeStruct(queries.shape, BF16),
            jax.ShapeDtypeStruct(passages.shape, BF16),
            jax.ShapeDtypeStruct((pairs, LANES), F32),
        ),
        in_specs=[pl.BlockSpec(memory_space=pltpu.SMEM), whole, whole, whole],
        out_specs=(whole, whole, whole),
        scratch_shapes=[
            vmem((slot_rows, width), BF16),
            vmem((slot_rows, width), BF16),
            vmem((slot_rows, width), BF16),
            vmem((peer_count // 2, (capacity + 1) * PBLK, width), BF16),
            vmem((peer_count // 2, (capacity + 1) * PBLK, width), BF16),
            vmem(passages.shape, F32),
            vmem((OWN, pairs, slot_rows, LANES), F32),
            vmem((OWN, slot_rows, LANES), F32),
            vmem((pairs, cand, LANES), jnp.int32),
            vmem((pairs, cand, LANES), F32),
            vmem((2, pairs, cand, LANES), F32),
            vmem((OWN, pairs, cand, LANES), F32),
            vmem((OWN, pairs, cand + PBLK, LANES), F32),
            vmem((OWN, pairs, cand + PBLK, LANES), BF16),
            vmem((OWN, slot_rows, query_count), BF16),
            vmem((OWN, slot_rows, LANES), F32),
            vmem((OWN, 8, LANES), F32),
            vmem((OWN, 8, LANES), F32),
            vmem((smalls, LANES), F32),
            vmem((2, smalls, LANES), F32),
            vmem((smalls, LANES), F32),
            vmem((4, smalls, LANES), F32),
            dma((peer_count,)), dma((peer_count,)), dma((peer_count,)), dma((peer_count,)),
            dma((pairs,)), dma((2, pairs)), dma((1,)), dma((2,)),
            dma((2, pairs)), dma((pairs,)), dma((4,)), dma((4,)),
        ],
        compiler_params=pltpu.CompilerParams(
            collective_id=0, has_side_effects=True, vmem_limit_bytes=56 * 2**20
        ),
        name="matryoshka",
    )(table, positives.reshape(pairs, LANES), queries, passages)
    results = (query_grad, passage_grad, loss)
    anywhere = pl.BlockSpec(memory_space=pl.ANY)
    query_grad, passage_grad, loss = pl.pallas_call(
        copy_out,
        out_shape=tuple(jax.ShapeDtypeStruct(part.shape, part.dtype) for part in results),
        in_specs=[anywhere] * 3,
        out_specs=(anywhere,) * 3,
        scratch_shapes=[dma((3,))],
        name="copy_out",
    )(*results)
    return query_grad, passage_grad, loss.reshape(query_count)


def solution(mesh):
    return jax.shard_map(
        per_device,
        mesh=mesh,
        in_specs=(P("dp", "tensor"), P("dp", "tensor"), P(), P("dp")),
        out_specs=(P("dp", "tensor"), P("dp", "tensor"), P("dp")),
        check_vma=False,
    )
```

```python
from functools import partial

import jax
import jax.numpy as jnp
from jax import lax
from jax.experimental import pallas as pl
from jax.experimental.pallas import tpu as pltpu
from jax.sharding import PartitionSpec as P

MINP = 64
NPRE = 7
PBLK = 16
QBLK = 64
LANES = 128
OWN = 5

EPS = 1e-06
INV_TEMP = 20.0
MESH = pl.DeviceIdType.MESH
F32 = jnp.float32
BF16 = jnp.bfloat16


def request_plan(flat_ids, capacity, per_owner):
    entry_count = flat_ids.shape[0]
    is_valid = flat_ids >= 0
    entry_order = jnp.arange(entry_count, dtype=jnp.int32)
    earlier = entry_order[None, :] < entry_order[:, None]
    same_block = (flat_ids[:, None] == flat_ids[None, :]) & is_valid[None, :]
    is_first = is_valid & jnp.logical_not(jnp.any(same_block & earlier, axis=1))
    owner_index = jnp.where(is_valid, flat_ids // per_owner, 0)
    local_block = jnp.where(is_valid, flat_ids % per_owner, 0)
    owner_rank = jnp.sum(
        ((owner_index[:, None] == owner_index[None, :]) & earlier & is_first[None, :]).astype(
            jnp.int32
        ),
        axis=1,
    )
    home_slot = jnp.where(is_first, owner_index * capacity + owner_rank, 0)
    entry_slot = jnp.sum(jnp.where(same_block & is_first[None, :], home_slot[None, :], 0), axis=1)
    return (is_first, home_slot, entry_slot, local_block)


def dot_nt(left, right):
    return lax.dot_general(left, right, (((1,), (1,)), ((), ())), preferred_element_type=F32)


def dot_tn(left, right):
    return lax.dot_general(left, right, (((0,), (0,)), ((), ())), preferred_element_type=F32)


def partner(me, step, peers):
    other, digit = 0, 1
    while digit < peers:
        other = other + lax.rem(lax.div(me, digit) + lax.div(step, digit), 2) * digit
        digit *= 2
    return other


def to_row(column):
    return column.T[0:1, :]


def to_column(row):
    return jnp.broadcast_to(row, (LANES, LANES)).T


def kernel(
    peers, cap, blocks, neg, local_blocks,
    tab, pos_ref, q_ref, p_ref, dq_ref, dp_ref, loss_ref,
    panels, sendbuf, gradbuf, near, far, total_grad, dots, psq, cid, gathered, got, coef, terms, half,
    grid, cols, qsq, rows, small, got_small, back, got_back,
    send1, recv1, send2, recv2, dg_send, dg_recv, sm_send, sm_recv, cf_send, cf_recv,
    sb_send, sb_recv,
):
    me, shard = lax.axis_index("dp"), lax.axis_index("tensor")
    width = q_ref.shape[1]
    chunk = cap * PBLK
    slots = peers * cap
    pairs = blocks // 2
    cand = neg * PBLK
    tiles = slots * PBLK // LANES
    want_at = 0
    slot_at = want_at + slots
    id_at = slot_at + blocks * neg
    ent_at = id_at + blocks * neg
    inv_at = ent_at + blocks * slots
    last = OWN - 1

    barrier = pltpu.get_barrier_semaphore()

    def greet(step, carry):
        pl.semaphore_signal(
            barrier, inc=1, device_id={"dp": lax.rem(me + step, peers)}, device_id_type=MESH
        )
        return carry

    lax.fori_loop(1, peers, greet, 0)
    for step in range(1, 4):
        pl.semaphore_signal(
            barrier, inc=1, device_id={"tensor": lax.rem(shard + step, 4)}, device_id_type=MESH
        )

    def pack(peer, target, offset):
        for k in range(cap):
            block = tab[want_at + peer * cap + k]
            target[pl.ds(offset + k * PBLK, PBLK), :] = p_ref[pl.ds(block * PBLK, PBLK), :]

    def chunk_rows(peer):
        return pl.ds(pl.multiple_of(peer * chunk, PBLK), chunk)

    def fetch(peer):
        return pltpu.make_async_remote_copy(
            src_ref=sendbuf.at[chunk_rows(peer)],
            dst_ref=panels.at[chunk_rows(me)],
            send_sem=send1.at[peer],
            recv_sem=recv1.at[me],
            device_id={"dp": peer},
            device_id_type=MESH,
        )

    def fetched(peer):
        return pltpu.make_async_remote_copy(
            src_ref=sendbuf.at[chunk_rows(me)],
            dst_ref=panels.at[chunk_rows(peer)],
            send_sem=send1.at[me],
            recv_sem=recv1.at[peer],
            device_id={"dp": peer},
            device_id_type=MESH,
        )

    pl.semaphore_wait(barrier, peers - 1 + 3)

    def start_fetch(step, carry):
        peer = partner(me, peers - step, peers)
        pack(peer, sendbuf, pl.multiple_of(peer * chunk, PBLK))
        fetch(peer).start()
        return carry

    lax.fori_loop(1, peers, start_fetch, 0)
    pack(me, panels, pl.multiple_of(me * chunk, PBLK))

    low_half = lax.broadcasted_iota(jnp.int32, (PBLK, LANES), 1) < QBLK
    low_row = lax.broadcasted_iota(jnp.int32, (1, LANES), 1) < QBLK

    def query_terms(j, carry):
        block = q_ref[pl.ds(pl.multiple_of(j * LANES, LANES), LANES), :].astype(F32)
        square = block * block

        def put(k, value):
            qsq[k, pl.ds(j, 1), :] = to_row(jnp.broadcast_to(value, (LANES, LANES)))

        prefix_squares(square, put)
        for e in range(neg):
            low = tab[id_at + (2 * j) * neg + e]
            high = tab[id_at + (2 * j + 1) * neg + e]
            cid[j, e * PBLK : (e + 1) * PBLK, :] = jnp.where(
                low_half, low, high
            ) * PBLK + lax.broadcasted_iota(jnp.int32, (PBLK, LANES), 0)
        return carry

    def prefix_squares(square, put):
        @pl.when(shard == 0)
        def _():
            first = square[:, :LANES]
            total = jnp.sum(jnp.where(low_row, first, 0.0), axis=1, keepdims=True)
            put(0, total)
            total = jnp.sum(first, axis=1, keepdims=True)
            put(1, total)
            for k in range(2, OWN):
                total = total + jnp.sum(
                    square[:, MINP * 2 ** (k - 1) : MINP * 2**k], axis=1, keepdims=True
                )
                put(k, total)

        @pl.when(shard != 0)
        def _():
            put(last, jnp.sum(square, axis=1, keepdims=True))

    lax.fori_loop(0, pairs, query_terms, 0)

    for k in range(OWN):
        half[k, :, cand : cand + PBLK, :] = jnp.zeros((pairs, PBLK, LANES), BF16)
        terms[k, :, cand : cand + PBLK, :] = jnp.zeros((pairs, PBLK, LANES), F32)
    back[...] = jnp.zeros_like(back)
    small[...] = jnp.zeros_like(small)

    def forward(step, carry):
        peer = partner(me, lax.rem(peers - step, peers), peers)

        @pl.when(step > 0)
        def _():
            fetched(peer).wait_recv()

        here = chunk_rows(peer)
        square = panels[here, :].astype(F32)
        square = square * square

        def put(k, value):
            psq[k, here, :] = jnp.broadcast_to(value, (chunk, LANES))

        prefix_squares(square, put)

        def keep(k, value):
            for j in range(pairs):
                dots[k, j, here, :] = value[:, j * LANES : (j + 1) * LANES]

        @pl.when(shard == 0)
        def _():
            first, query = panels[here, :LANES], q_ref[:, :LANES]
            keep(0, dot_nt(jnp.where(low_row, first, jnp.zeros((), BF16)), query))
            total = dot_nt(first, query)
            keep(1, total)
            for k in range(2, OWN):
                span = slice(MINP * 2 ** (k - 1), MINP * 2**k)
                total = total + dot_nt(panels[here, span], q_ref[:, span])
                keep(k, total)

        @pl.when(shard != 0)
        def _():
            keep(last, dot_nt(panels[here, :], q_ref[...]))

        if chunk == LANES:
            small[pl.ds(peer, 1), :] = to_row(psq[last, here, :])
        return carry

    lax.fori_loop(0, peers, forward, 0)

    def pick(ref, k, j, lead):
        parts = []
        for e in range(neg):
            low = tab[slot_at + (2 * j) * neg + e] * PBLK
            high = tab[slot_at + (2 * j + 1) * neg + e] * PBLK
            low = ref[lead(k, j) + (pl.ds(low, PBLK),)]
            high = ref[lead(k, j) + (pl.ds(high, PBLK),)]
            parts.append(jnp.where(low_half, low, high))
        return jnp.concatenate(parts, axis=0)

    def pick_dots(k, j):
        return pick(dots, k, j, lambda k, j: (k, j))

    def pick_squares(k, j):
        return pick(psq, k, j, lambda k, j: (k,))

    def small_copy(target, slot):
        return pltpu.make_async_remote_copy(
            src_ref=small, dst_ref=got_small.at[slot], send_sem=sm_send.at[0],
            recv_sem=sm_recv.at[slot], device_id={"tensor": target}, device_id_type=MESH,
        )

    def dots_copy(target, slot, j):
        return pltpu.make_async_remote_copy(
            src_ref=gathered.at[j], dst_ref=got.at[slot, j], send_sem=dg_send.at[j],
            recv_sem=dg_recv.at[slot, j], device_id={"tensor": target}, device_id_type=MESH,
        )

    def later_copy(j):
        return pltpu.make_async_remote_copy(
            src_ref=coef.at[last, j], dst_ref=got.at[0, j], send_sem=cf_send.at[0, j],
            recv_sem=dg_recv.at[0, j], device_id={"tensor": 0}, device_id_type=MESH,
        )

    def half_copy(target, j):
        return pltpu.make_async_remote_copy(
            src_ref=half.at[last, j, pl.ds(0, cand)], dst_ref=half.at[last, j, pl.ds(0, cand)],
            send_sem=cf_send.at[target - 1, j], recv_sem=cf_recv.at[j],
            device_id={"tensor": target}, device_id_type=MESH,
        )

    for t in range(tiles if chunk != LANES else 0):
        small[t : t + 1, :] = to_row(psq[last, t * LANES : (t + 1) * LANES, :])
    small[tiles : tiles + pairs, :] = qsq[last, 0:pairs, :]

    def widen():
        for t in range(tiles):
            psq[last, t * LANES : (t + 1) * LANES, :] = to_column(small[t : t + 1, :])
        qsq[last, 0:pairs, :] = small[tiles : tiles + pairs, :]

    def each_pair(body):
        def step(j, carry):
            body(j)
            return carry

        lax.fori_loop(0, pairs, step, 0)

    def prefix_terms(products, squares, k, j, weight):
        number = cid[j]
        live = number >= 0
        query_scale = lax.rsqrt(qsq[k, pl.ds(j, 1), :] + EPS)
        passage_scale = jnp.where(live, lax.rsqrt(squares + EPS), 0.0)
        scale = query_scale * passage_scale * INV_TEMP
        logits = products * scale
        exponent = jnp.where(live, jnp.exp(logits), 0.0)
        total = jnp.sum(exponent, axis=0, keepdims=True)
        hit = number == pos_ref[pl.ds(j, 1), :]
        loss = jnp.log(total) - jnp.sum(jnp.where(hit, logits, 0.0), axis=0, keepdims=True)
        gradient = weight * (exponent * (1.0 / total) - jnp.where(hit, 1.0, 0.0))
        inner = gradient * logits
        row = query_scale * query_scale * jnp.sum(inner, axis=0, keepdims=True)
        return gradient * scale, row, passage_scale * passage_scale * inner, weight * loss

    def one_prefix(products, j, weight):
        value, row, column, loss = prefix_terms(
            products, pick_squares(last, j), last, j, weight
        )
        coef[last, j] = value
        terms[last, j, 0:cand, :] = column
        rows[last, pl.ds(j, 1), :] = row
        back[pl.ds(tiles + pairs + j, 1), :] = loss

    def pick_half(ref, k, j, slot):
        low = tab[ent_at + (2 * j) * slots + slot] * PBLK
        high = tab[ent_at + (2 * j + 1) * slots + slot] * PBLK
        return jnp.where(
            low_half,
            ref[k, j, pl.ds(low, PBLK), :],
            ref[k, j, pl.ds(high, PBLK), :],
        )

    def column_sums(count):
        def step(slot, carry):
            for k in range(OWN - count, OWN):
                total = pick_half(terms, k, 0, slot)
                for j in range(1, pairs):
                    total = total + pick_half(terms, k, j, slot)
                cols[k, pl.ds(pl.multiple_of(slot * PBLK, PBLK), PBLK), :] = jnp.broadcast_to(
                    jnp.sum(total, axis=1, keepdims=True), (PBLK, LANES)
                )
            return carry

        lax.fori_loop(0, slots, step, 0)
        for t in range(tiles):
            back[t : t + 1, :] = to_row(cols[last, t * LANES : (t + 1) * LANES, :])
        back[tiles : tiles + pairs, :] = rows[last, 0:pairs, :]

    def back_copy(step, slot):
        return pltpu.make_async_remote_copy(
            src_ref=back, dst_ref=got_back.at[slot], send_sem=sb_send.at[step],
            recv_sem=sb_recv.at[slot], device_id={"tensor": lax.rem(shard + step, 4)},
            device_id_type=MESH,
        )

    def send_back():
        for step in range(1, 4):
            back_copy(step, shard).start()

    @pl.when(shard == 0)
    def _():
        small_copy(1, 0).start()

        def hand_on(j):
            gathered[j] = pick_dots(last, j)
            dots_copy(1, 0, j).start()

        each_pair(hand_on)

        def own(j):
            value = row = column = loss = None
            for k in reversed(range(OWN)):
                products = gathered[j] if k == last else pick_dots(k, j)
                part = prefix_terms(products, pick_squares(k, j), k, j, float(2**k))
                if k == last:
                    value, row, column, loss = part
                else:
                    value, row, column, loss = (
                        value + part[0], row + part[1], column + part[2], loss + part[3]
                    )
                coef[k, j] = value
                rows[k, pl.ds(j, 1), :] = row
                terms[k, j, 0:cand, :] = column
            back[pl.ds(tiles + pairs + j, 1), :] = loss

        each_pair(own)
        column_sums(OWN)
        send_back()

        def finish(j):
            later_copy(j).wait_recv()
            for k in range(OWN):
                half[k, j, 0:cand, :] = (coef[k, j] + got[0, j]).astype(BF16)

        each_pair(finish)
        small_copy(1, 0).wait_send()
        each_pair(lambda j: dots_copy(1, 0, j).wait_send())

    @pl.when(shard == 1)
    def _():
        small_copy(3, 0).wait_recv()
        small[...] = small[...] + got_small[0]
        small_copy(3, 0).start()

        def hand_on(j):
            dots_copy(3, 0, j).wait_recv()
            gathered[j] = pick_dots(last, j) + got[0, j]
            dots_copy(3, 0, j).start()

        each_pair(hand_on)
        widen()
        each_pair(lambda j: one_prefix(gathered[j], j, 32.0))
        column_sums(1)
        send_back()

        def finish(j):
            half_copy(1, j).wait_recv()
            total = coef[last, j] + half[last, j, 0:cand, :].astype(F32)
            coef[last, j] = total
            later_copy(j).start()
            half[last, j, 0:cand, :] = total.astype(BF16)

        each_pair(finish)
        small_copy(3, 0).wait_send()
        each_pair(lambda j: dots_copy(3, 0, j).wait_send())
        each_pair(lambda j: later_copy(j).wait_send())

    @pl.when(shard == 2)
    def _():
        small_copy(3, 1).start()

        def hand_on(j):
            gathered[j] = pick_dots(last, j)
            dots_copy(3, 1, j).start()

        each_pair(hand_on)
        cols[last] = jnp.zeros_like(cols[last])
        rows[last] = jnp.zeros_like(rows[last])
        send_back()
        each_pair(lambda j: half_copy(2, j).wait_recv())
        small_copy(3, 1).wait_send()
        each_pair(lambda j: dots_copy(3, 1, j).wait_send())

    @pl.when(shard == 3)
    def _():
        small_copy(2, 0).wait_recv()
        small_copy(2, 1).wait_recv()
        small[...] = small[...] + got_small[0] + got_small[1]
        widen()

        def answer(j):
            mine = pick_dots(last, j)
            dots_copy(2, 1, j).wait_recv()
            dots_copy(2, 0, j).wait_recv()
            one_prefix(mine + got[0, j] + got[1, j], j, 64.0)
            half[last, j, 0:cand, :] = coef[last, j].astype(BF16)
            half_copy(1, j).start()
            half_copy(2, j).start()

        each_pair(answer)
        column_sums(1)
        send_back()
        each_pair(lambda j: half_copy(1, j).wait_send())
        each_pair(lambda j: half_copy(2, j).wait_send())

    later = jnp.zeros(back.shape, F32)
    loss = back[tiles + pairs : tiles + 2 * pairs, :]
    for step in range(1, 4):
        other = lax.rem(shard + step, 4)
        back_copy(step, other).wait_recv()
        part = got_back[other]
        later = later + jnp.where(other > shard, 1.0, 0.0) * part
        loss = loss + part[tiles + pairs : tiles + 2 * pairs, :]
    weight_total = sum(2.0**k for k in range(NPRE))
    loss_ref[...] = loss / weight_total

    def add_later(count):
        for t in range(tiles):
            extra = to_column(later[t : t + 1, :])
            for k in range(OWN - count, OWN):
                cols[k, t * LANES : (t + 1) * LANES, :] += extra
        for k in range(OWN - count, OWN):
            rows[k, 0:pairs, :] += later[tiles : tiles + pairs, :]

    @pl.when(shard == 0)
    def _():
        add_later(OWN)

    @pl.when(shard != 0)
    def _():
        add_later(1)

    spans = [(k, slice(MINP * 2 ** (k - 1), MINP * 2**k)) for k in range(2, OWN)]

    def build(k, peer):
        def step(i, carry):
            slot = peer * cap + i
            for j in range(pairs):
                grid[
                    k, pl.ds(pl.multiple_of(slot * PBLK, PBLK), PBLK), j * LANES : (j + 1) * LANES
                ] = pick_half(half, k, j, slot)
            return carry

        lax.fori_loop(0, cap, step, 0)

    split = peers // 2

    def landing(step, is_far):
        return far.at[step - split] if is_far else near.at[step]

    def grad_copy(step, is_far):
        peer = partner(me, step, peers)
        return pltpu.make_async_remote_copy(
            src_ref=gradbuf.at[chunk_rows(peer)],
            dst_ref=landing(step, is_far).at[pl.ds(0, chunk)],
            send_sem=send2.at[step], recv_sem=recv2.at[step],
            device_id={"dp": peer}, device_id_type=MESH,
        )

    def passage_part(step):
        peer = partner(me, step, peers)
        here = chunk_rows(peer)

        def put(span, k, product):
            piece = product - cols[k, here, 0:1] * panels[here, span].astype(F32)
            gradbuf[here, span] = piece.astype(BF16)

        @pl.when(shard == 0)
        def _():
            for k in range(OWN):
                build(k, peer)
            query = q_ref[:, :LANES]
            first = panels[here, :LANES].astype(F32)
            low = jnp.dot(grid[0, here, :], query, preferred_element_type=F32)
            low = low - cols[0, here, :] * first
            high = jnp.dot(grid[1, here, :], query, preferred_element_type=F32)
            high = high - cols[1, here, :] * first
            gradbuf[here, :LANES] = jnp.where(low_row, low, high).astype(BF16)
            for k, span in spans:
                put(span, k, jnp.dot(grid[k, here, :], q_ref[:, span], preferred_element_type=F32))

        @pl.when(shard != 0)
        def _():
            build(last, peer)
            put(
                slice(0, width), last,
                jnp.dot(grid[last, here, :], q_ref[...], preferred_element_type=F32),
            )

    def far_part(i, carry):
        passage_part(peers - 1 - i)
        grad_copy(peers - 1 - i, True).start()
        return carry

    def near_part(i, carry):
        passage_part(split - i)
        grad_copy(split - i, False).start()
        return carry

    lax.fori_loop(0, split, far_part, 0)
    lax.fori_loop(1, split, near_part, 0)
    passage_part(0)
    near[0, 0:chunk, :] = gradbuf[chunk_rows(me), :]

    def query_part(k, span):
        column = jnp.concatenate(
            [to_column(rows[k, j : j + 1, :])[:, 0:1] for j in range(pairs)], axis=0
        )
        return dot_tn(grid[k], panels[:, span]) - column * q_ref[:, span].astype(F32)

    @pl.when(shard == 0)
    def _():
        first = slice(0, LANES)
        piece = jnp.where(low_row, query_part(0, first), query_part(1, first))
        dq_ref[:, first] = piece.astype(BF16)
        for k, span in spans:
            dq_ref[:, span] = query_part(k, span).astype(BF16)

    @pl.when(shard != 0)
    def _():
        for start in range(0, width, 2 * LANES):
            span = slice(start, start + 2 * LANES)
            dq_ref[:, span] = query_part(last, span).astype(BF16)

    zeros = jnp.zeros((split, PBLK, width), BF16)
    near[:, chunk : chunk + PBLK, :] = zeros
    far[:, chunk : chunk + PBLK, :] = zeros

    def add_up(ref, first, block, total):
        def add(i, total):
            peer = partner(me, first + i, peers)
            row = tab[inv_at + peer * local_blocks + block] * PBLK
            return total + ref[i, pl.ds(row, PBLK), :].astype(F32)

        return lax.fori_loop(0, split, add, total)

    def block_rows(block):
        return pl.ds(pl.multiple_of(block * PBLK, PBLK), PBLK)

    def drain_near(step, carry):
        grad_copy(step, False).wait_recv()
        return carry

    def near_block(block, carry):
        total_grad[block_rows(block), :] = add_up(near, 0, block, jnp.zeros((PBLK, width), F32))
        return carry

    def drain_far(i, carry):
        grad_copy(split + i, True).wait_recv()
        return carry

    def far_block(block, carry):
        total = add_up(far, split, block, total_grad[block_rows(block), :])
        dp_ref[block_rows(block), :] = total.astype(BF16)
        return carry

    lax.fori_loop(1, split, drain_near, 0)
    lax.fori_loop(0, local_blocks, near_block, 0)
    lax.fori_loop(0, split, drain_far, 0)
    lax.fori_loop(0, local_blocks, far_block, 0)

    def sent(step, carry):
        fetch(partner(me, step, peers)).wait_send()
        return carry

    def near_sent(step, carry):
        grad_copy(step, False).wait_send()
        return carry

    def far_sent(i, carry):
        grad_copy(split + i, True).wait_send()
        return carry

    lax.fori_loop(1, peers, sent, 0)
    lax.fori_loop(1, split, near_sent, 0)
    lax.fori_loop(0, split, far_sent, 0)
    for step in range(1, 4):
        back_copy(step, shard).wait_send()


def copy_out(*refs):
    sources, targets, held, arrived, left = refs[:3], refs[3:6], refs[6:9], refs[9], refs[10]
    parts, number = [], 0
    for source, target, hold in zip(sources, targets, held):
        count = source.shape[0]
        step = min(count, LANES)
        for start in range(0, count, step):
            part = pl.ds(start, step)
            parts.append((
                pltpu.make_async_copy(source.at[part], hold.at[part], arrived.at[number]),
                pltpu.make_async_copy(hold.at[part], target.at[part], left.at[number]),
            ))
            number += 1
    for arrive, leave in parts:
        arrive.start()
    for arrive, leave in parts:
        arrive.wait()
        leave.start()
    for arrive, leave in parts:
        leave.wait()


def per_device(queries, passages, neg_lists, positives):
    peer_count = lax.axis_size("dp")
    width = queries.shape[1]
    blocks_here = neg_lists.shape[0] // peer_count
    neg_count = neg_lists.shape[1]
    local_blocks = passages.shape[0] // PBLK
    capacity = blocks_here * neg_count // 2 // peer_count
    slot_count = peer_count * capacity
    cand = neg_count * PBLK
    pairs = blocks_here // 2
    my_index = lax.axis_index("dp")
    flat_all = neg_lists.reshape(peer_count, blocks_here * neg_count)
    is_first, home_slot, entry_slot, local_block = jax.vmap(
        partial(request_plan, capacity=capacity, per_owner=local_blocks)
    )(flat_all)
    targets = my_index * capacity + jnp.arange(capacity, dtype=jnp.int32)
    target_hit = is_first[:, :, None] & (home_slot[:, :, None] == targets[None, None, :])
    wanted = jnp.sum(jnp.where(target_hit, local_block[:, :, None] + 1, 0), axis=1) - 1
    own_ids = lax.dynamic_index_in_dim(flat_all, my_index, 0, keepdims=False)
    own_slot = lax.dynamic_index_in_dim(entry_slot, my_index, 0, keepdims=False)
    own_live = own_ids >= 0
    entries = jnp.arange(neg_count, dtype=jnp.int32)[None, :, None]
    at_slot = (
        own_slot.reshape(blocks_here, neg_count, 1) == jnp.arange(slot_count, dtype=jnp.int32)
    ) & own_live.reshape(blocks_here, neg_count, 1)
    entry_of = neg_count + jnp.sum(jnp.where(at_slot, entries - neg_count, 0), axis=1)
    named = wanted[:, :, None] == jnp.arange(local_blocks, dtype=jnp.int32)
    ranks = jnp.arange(capacity, dtype=jnp.int32)[None, :, None]
    rank_of = capacity + jnp.sum(jnp.where(named, ranks - capacity, 0), axis=1)
    table = jnp.concatenate([
        jnp.maximum(wanted, 0).reshape(-1),
        jnp.where(own_live, own_slot, 0),
        jnp.where(own_live, own_ids, -1),
        entry_of.reshape(-1),
        rank_of.reshape(-1),
    ]).astype(jnp.int32)

    slot_rows = slot_count * PBLK
    query_count = queries.shape[0]
    smalls = slot_rows // LANES + 2 * pairs
    vmem, dma = pltpu.VMEM, pltpu.SemaphoreType.DMA
    whole = pl.BlockSpec(memory_space=pltpu.VMEM)
    query_grad, passage_grad, loss = pl.pallas_call(
        partial(kernel, peer_count, capacity, blocks_here, neg_count, local_blocks),
        out_shape=(
            jax.ShapeDtypeStruct(queries.shape, BF16),
            jax.ShapeDtypeStruct(passages.shape, BF16),
            jax.ShapeDtypeStruct((pairs, LANES), F32),
        ),
        in_specs=[pl.BlockSpec(memory_space=pltpu.SMEM), whole, whole, whole],
        out_specs=(whole, whole, whole),
        scratch_shapes=[
            vmem((slot_rows, width), BF16),
            vmem((slot_rows, width), BF16),
            vmem((slot_rows, width), BF16),
            vmem((peer_count // 2, (capacity + 1) * PBLK, width), BF16),
            vmem((peer_count // 2, (capacity + 1) * PBLK, width), BF16),
            vmem(passages.shape, F32),
            vmem((OWN, pairs, slot_rows, LANES), F32),
            vmem((OWN, slot_rows, LANES), F32),
            vmem((pairs, cand, LANES), jnp.int32),
            vmem((pairs, cand, LANES), F32),
            vmem((2, pairs, cand, LANES), F32),
            vmem((OWN, pairs, cand, LANES), F32),
            vmem((OWN, pairs, cand + PBLK, LANES), F32),
            vmem((OWN, pairs, cand + PBLK, LANES), BF16),
            vmem((OWN, slot_rows, query_count), BF16),
            vmem((OWN, slot_rows, LANES), F32),
            vmem((OWN, 8, LANES), F32),
            vmem((OWN, 8, LANES), F32),
            vmem((smalls, LANES), F32),
            vmem((2, smalls, LANES), F32),
            vmem((smalls, LANES), F32),
            vmem((4, smalls, LANES), F32),
            dma((peer_count,)), dma((peer_count,)), dma((peer_count,)), dma((peer_count,)),
            dma((pairs,)), dma((2, pairs)), dma((1,)), dma((2,)),
            dma((2, pairs)), dma((pairs,)), dma((4,)), dma((4,)),
        ],
        compiler_params=pltpu.CompilerParams(
            collective_id=0, has_side_effects=True, vmem_limit_bytes=56 * 2**20
        ),
        name="matryoshka",
    )(table, positives.reshape(pairs, LANES), queries, passages)
    results = (query_grad, passage_grad, loss)
    pieces = sum(-(-part.shape[0] // LANES) for part in results)
    anywhere = pl.BlockSpec(memory_space=pl.ANY)
    query_grad, passage_grad, loss = pl.pallas_call(
        copy_out,
        out_shape=tuple(jax.ShapeDtypeStruct(part.shape, part.dtype) for part in results),
        in_specs=[anywhere] * 3,
        out_specs=(anywhere,) * 3,
        scratch_shapes=[vmem(part.shape, part.dtype) for part in results]
        + [dma((pieces,)), dma((pieces,))],
        name="copy_out",
    )(*results)
    return query_grad, passage_grad, loss.reshape(query_count)


def solution(mesh):
    return jax.shard_map(
        per_device,
        mesh=mesh,
        in_specs=(P("dp", "tensor"), P("dp", "tensor"), P(), P("dp")),
        out_specs=(P("dp", "tensor"), P("dp", "tensor"), P("dp")),
        check_vma=False,
    )
```
